32 devices in a mesh: seq: 8 (over z, x), head: 4 (over y, core).
Axes of the slice: x: 2, y: 2, z: 4, core: 2. Of those that a mesh axis runs over, the one named last changes fastest.
Arguments:
- queries: float32 [2048, 4096], P('seq', 'head'), may hold values from -0.54 to 0.54
- key_input: float32 [2048, 4096], P('seq', 'head'), may hold values from -0.54 to 0.54
- value_input: float32 [2048, 4096], P('seq', 'head'), may hold values from -6 to 6
- grad_output: float32 [2048, 4096], P('seq', 'head'), may hold values from -0.54 to 0.54
- log_decay: float32 [2048, 32], P('seq', 'head'), may hold values from -2 to 0
- level_weight: float32 [2048, 7], P('seq'), may hold values from 0.3 to 1.5
- segment: int32 [2048], P('seq'), may hold values from 0 to 3, never falling along the last dimension, each value on 1 to 1024 neighbouring positions
Outputs:
- grad_query: float32 [2048, 4096], P('seq', 'head')
- grad_key: float32 [2048, 4096], P('seq', 'head')
- grad_value: float32 [2048, 4096], P('seq', 'head')
- grad_level: float32 [2048, 7], P('seq')
The draws below stay inside these ranges and needn't reach their ends.
Inputs may be any that keep to these rules, and one draw needn't show every extreme that they name: `segment`: document numbers never fall along the tokens; each document has at most 1024 tokens, one exactly that many.
All inputs are finite; a program needn't handle non-finite values.
Results may differ from the reference program's by a relative error of at most 0.00012.
Values sent between devices are 32-bit elements; how exact they have to be, the bound alone decides.
No kernel may reach another device: no remote copies, remote signals or barrier semaphores. Data moves between devices by JAX's collectives and lax.ppermute only.
A program may use at most 128 MiB of HBM per device.

```python
import math
import jax
import jax.numpy as jnp
import numpy as np
from jax import lax

HEAD_TOTAL = 32
HEAD_DIM = 128
STRETCH = 256
LEVELS = 7
NDOC = 4
D = 4096
TOKEN_TOTAL = 2048
NB = 3


def draw_log_decay(key, part):
    fragment_list = jax.random.split(key, 7)
    fast_share = 0.5
    fast_heads = jax.random.uniform(fragment_list[0], (HEAD_TOTAL,)) < fast_share
    fast_rate = jnp.exp(jax.random.uniform(fragment_list[1], (HEAD_TOTAL,), minval=jnp.log(0.02), maxval=jnp.log(0.04)))
    slow_rate = jnp.exp(jax.random.uniform(fragment_list[2], (HEAD_TOTAL,), minval=jnp.log(0.02), maxval=jnp.log(0.2))) / TOKEN_TOTAL
    decay_rate = jnp.where(fast_heads, fast_rate, slow_rate)
    block_factor = jax.random.uniform(fragment_list[3], (TOKEN_TOTAL // STRETCH, HEAD_TOTAL), minval=0.5, maxval=2.0)
    token_factor = jax.random.uniform(fragment_list[4], (TOKEN_TOTAL, HEAD_TOTAL), minval=0.5, maxval=2.0)
    stable_mode = -decay_rate[None, :] * jnp.repeat(block_factor, STRETCH, axis=0) * token_factor
    flush_location = jax.random.randint(fragment_list[5], (2, HEAD_TOTAL), 0, TOKEN_TOTAL)
    flush_depth = jax.random.uniform(fragment_list[6], (2, HEAD_TOTAL), minval=0.22, maxval=0.69)
    token_offsets = jnp.arange(TOKEN_TOTAL, dtype=jnp.int32)[:, None, None]
    flush_events = jnp.sum(jnp.where(token_offsets == flush_location[None], flush_depth[None], 0.0), axis=1)
    return (stable_mode - flush_events).astype(jnp.float32)


def steps_of(rng, dims, pieces, low, high):
    def one(dim, blocks):
        steps = jax.random.uniform(jax.random.fold_in(jax.random.fold_in(rng, 6), dim), (blocks,), jnp.float32, low / len(pieces), high / len(pieces))
        return jnp.repeat(jnp.exp(steps), dims[dim] // blocks).reshape((-1,) + (1,) * (len(dims) - dim - 1))

    factor_of = one(*pieces[0])
    for cut in pieces[1:]:
        factor_of = factor_of * one(*cut)
    return factor_of


def profile(count, total, reach, lean):
    portions = [(1 << 20) // math.isqrt(grade ** lean) + 1 for grade in range(2, count + 1)]
    surplus, holding = total - reach - (count - 1), [1] * (count - 1)
    while surplus > 0:
        candidates = [i for i in range(count - 1) if holding[i] < reach]
        pool, left = sum([portions[i] for i in candidates]), surplus
        for i in candidates:
            addition = min(reach - holding[i], max(1, left * portions[i] // pool), surplus)
            holding[i] = holding[i] + addition
            surplus = surplus - addition
    return np.array([reach] + holding)


def uneven_parts(own_key, count, total, bound, skew):
    if count == 2:
        one = jax.random.randint(own_key, (), max(1, total - bound), min(bound, total - 1) + 1)
        return jnp.stack([one, total - one])
    tallies = jnp.asarray(profile(count, total, bound, skew), jnp.int32)
    twos = (count - 1) // 2
    source_of, receiver = tallies[1:1 + 2 * twos:2], tallies[2:2 + 2 * twos:2]
    margin = jnp.minimum(source_of - 1, bound - receiver)
    moved = jax.random.randint(jax.random.fold_in(own_key, 1), (twos,), 0, 1 << 20) % (margin + 1)
    tallies = tallies.at[1:1 + 2 * twos:2].set(source_of - moved).at[2:2 + 2 * twos:2].set(receiver + moved)
    return tallies[jax.random.permutation(jax.random.fold_in(own_key, 2), count)]


def noise(stream_key, shape, deviation, reach, pieces=(), kind=jnp.bfloat16):
    loudness = steps_of(stream_key, shape, pieces, -0.22, 0.18) if pieces else 1.0
    array = jax.random.normal(stream_key, shape, jnp.float32) * deviation * loudness
    return jnp.minimum(jnp.maximum(array, -reach), reach).astype(kind)


def setup_inputs(seed: int = 0) -> dict:
    key_list = jax.random.split(jax.random.key(seed), 8)
    queries = noise(key_list[0], (TOKEN_TOTAL, D), 0.09, 0.54, ((0, 8), (1, 4)), jnp.float32)
    key_input = noise(key_list[1], (TOKEN_TOTAL, D), 0.09, 0.54, ((0, 8), (1, 4)), jnp.float32)
    value_input = noise(key_list[2], (TOKEN_TOTAL, D), 1.0, 6.0, ((0, 8), (1, 4)), jnp.float32)
    grad_output = noise(key_list[3], (TOKEN_TOTAL, D), 0.09, 0.54, ((0, 8), (1, 4)), jnp.float32)
    log_decay = draw_log_decay(jax.random.fold_in(key_list[7], 71), 0)
    level_weight = jnp.clip(jnp.exp(math.log(1.5) - 1.60943787 * jax.random.uniform(key_list[5], (TOKEN_TOTAL, LEVELS), jnp.float32) ** steps_of(key_list[5], (TOKEN_TOTAL, LEVELS), ((0, 8),), -0.2, 0.2)), 0.3, 1.5)
    segment = jnp.searchsorted(jnp.cumsum(uneven_parts(key_list[6], NDOC, TOKEN_TOTAL, TOKEN_TOTAL // 2, 0)), jnp.arange(TOKEN_TOTAL), side="right").astype(jnp.int32)
    return {"queries": queries, "key_input": key_input, "value_input": value_input, "grad_output": grad_output, "log_decay": log_decay, "level_weight": level_weight, "segment": segment}


PRECISE = lax.Precision.HIGHEST


def stretch_spans(totals):
    stretches = totals.shape[0]
    stretch_ids = jnp.arange(stretches, dtype=jnp.int32)
    inside = (stretch_ids[None, None, :] > stretch_ids[:, None, None]) & (stretch_ids[None, None, :] <= stretch_ids[None, :, None])
    return jnp.sum(jnp.where(inside, totals[None, None, :], 0.0), axis=2)


def head_grads(queries, key_input, value_input, grad_output, log_decay, level_weight, segment):
    stretches = queries.shape[0]
    cumulative = jnp.cumsum(log_decay, axis=1)
    totals = cumulative[:, -1]
    stretch_ends = segment[:, -1]
    spans = stretch_spans(totals)
    position = jnp.arange(STRETCH, dtype=jnp.int32)
    visible = (position[None, :, None] >= position[None, None, :]) & (segment[:, :, None] == segment[:, None, :])
    decay_gap = cumulative[:, :, None] - cumulative[:, None, :]
    within = jnp.where(visible, jnp.exp(jnp.minimum(decay_gap, 0.0)), 0.0)
    scores = jnp.einsum('ctd,csd->cts', queries, key_input, precision=PRECISE)
    grad_scores = jnp.einsum('ctd,csd->cts', grad_output, value_input, precision=PRECISE)
    weight = within * level_weight[:, :, 0][:, :, None]
    head_value = jnp.einsum('cts,ctd->csd', weight * scores, grad_output, precision=PRECISE)
    head_query = jnp.einsum('cts,csd->ctd', weight * grad_scores, key_input, precision=PRECISE)
    head_key = jnp.einsum('cts,ctd->csd', weight * grad_scores, queries, precision=PRECISE)
    level_grads = [jnp.sum(within * scores * grad_scores, axis=2)]
    source_weight = jnp.exp(totals[:, None] - cumulative) * (segment == stretch_ends[:, None]).astype(jnp.float32)
    states = jnp.einsum('csi,csj->cij', source_weight[:, :, None] * key_input, value_input, precision=PRECISE)
    stretch_ids = jnp.arange(stretches, dtype=jnp.int32)
    grad_states = jnp.zeros_like(states)
    for level in range(1, NB + 1):
        half_size = 1 << (level - 1)
        upper_half = ((stretch_ids >> (level - 1)) & 1) == 1
        lower_end = ((stretch_ids >> level) << level) + half_size - 1
        member = upper_half[:, None] & (stretch_ids[None, :] >= lower_end[:, None] - half_size + 1) & (stretch_ids[None, :] <= lower_end[:, None])
        source_span = spans[:, lower_end].T
        linked = member & (stretch_ends[None, :] == stretch_ends[lower_end][:, None])
        carried = jnp.where(linked, jnp.exp(jnp.where(linked, source_span, 0.0)), 0.0)
        blocks = jnp.einsum('cx,xij->cij', carried, states, precision=PRECISE)
        before = jnp.maximum(stretch_ids - 1, 0)
        query_span = spans[lower_end, before]
        factor = jnp.where(upper_half[:, None] & (segment == stretch_ends[lower_end][:, None]), jnp.exp(cumulative + query_span[:, None]), 0.0)
        level_scale = factor * level_weight[:, :, level]
        head_query = head_query + level_scale[:, :, None] * jnp.einsum('ctj,cij->cti', grad_output, blocks, precision=PRECISE)
        reached = jnp.einsum('cti,cij->ctj', queries, blocks, precision=PRECISE)
        level_grads.append(factor * jnp.sum(reached * grad_output, axis=2))
        grad_blocks = jnp.einsum('cti,ctj->cij', level_scale[:, :, None] * queries, grad_output, precision=PRECISE)
        grad_states = grad_states + jnp.einsum('cx,cij->xij', carried, grad_blocks, precision=PRECISE)
    head_key = head_key + source_weight[:, :, None] * jnp.einsum('csj,cij->csi', value_input, grad_states, precision=PRECISE)
    head_value = head_value + source_weight[:, :, None] * jnp.einsum('csi,cij->csj', key_input, grad_states, precision=PRECISE)
    for level in range(NB + 1, LEVELS):
        level_grads.append(jnp.zeros_like(level_grads[0]))
    return head_query, head_key, head_value, jnp.stack(level_grads, axis=2)


def reference(queries, key_input, value_input, grad_output, log_decay, level_weight, segment):
    stretches = TOKEN_TOTAL // STRETCH

    def split_heads(tensor):
        return tensor.reshape(stretches, STRETCH, HEAD_TOTAL, HEAD_DIM).transpose(2, 0, 1, 3)

    def merge_heads(tensor):
        return tensor.transpose(1, 2, 0, 3).reshape(TOKEN_TOTAL, HEAD_TOTAL * HEAD_DIM)

    decay_heads = log_decay.reshape(stretches, STRETCH, HEAD_TOTAL).transpose(2, 0, 1)
    weight_rows = level_weight.reshape(stretches, STRETCH, LEVELS)
    segment_rows = segment.reshape(stretches, STRETCH)

    def one_head(head_items):
        return head_grads(head_items[0], head_items[1], head_items[2], head_items[3], head_items[4], weight_rows, segment_rows)

    head_query, head_key, head_value, head_level = lax.map(one_head, (split_heads(queries), split_heads(key_input), split_heads(value_input), split_heads(grad_output), decay_heads))
    grad_level = jnp.sum(head_level, axis=0).reshape(TOKEN_TOTAL, LEVELS)
    return merge_heads(head_query), merge_heads(head_key), merge_heads(head_value), grad_level
```

```python
import functools

import jax
import jax.numpy as jnp
from jax import lax
from jax.experimental import pallas as pl
from jax.experimental.pallas import tpu as pltpu
from jax.sharding import PartitionSpec as P

HIGH = lax.Precision.HIGH
EXACT = lax.Precision.HIGHEST
LANES = 128
PARTS = 2
VMEM_LIMIT = 40 * 1024 * 1024


def dot(a, b, over, precision=HIGH):
    return lax.dot_general(
        a, b, (over, ((), ())), precision=precision, preferred_element_type=jnp.float32
    )


def params(steps):
    return pltpu.CompilerParams(
        dimension_semantics=("arbitrary",) * steps, vmem_limit_bytes=VMEM_LIMIT
    )


def cost(flops, moved):
    return pl.CostEstimate(flops=int(flops), bytes_accessed=int(moved), transcendentals=0)


def lane_of(shape):
    return lax.broadcasted_iota(jnp.int32, shape, len(shape) - 1)


def prepare_kernel(heads, decay_ref, segment_ref, cols_ref, rows_ref, table_ref):
    tokens = decay_ref.shape[0]
    head = lax.broadcasted_iota(jnp.int32, (heads, LANES), 0)
    lane = lane_of((heads, LANES))
    spread = ((lane < 3 * heads) & (lax.rem(lane, heads) == head)).astype(jnp.float32)
    wide = dot(decay_ref[...], spread, ((1,), (0,)), EXACT)
    earlier = lax.broadcasted_iota(jnp.int32, (tokens, tokens), 0) >= lane_of((tokens, tokens))
    running = dot(earlier.astype(jnp.float32), wide, ((1,), (0,)), EXACT)
    document = jnp.broadcast_to(segment_ref[...].astype(jnp.float32), (LANES, tokens)).T
    total, first, last = running[tokens - 1 :], document[:1], document[tokens - 1 :]
    source = jnp.exp(total - running) * (document == last).astype(jnp.float32)
    query = jnp.exp(running) * (document == first).astype(jnp.float32)
    lane = lane_of((tokens, LANES))
    cols = jnp.where(
        lane < heads,
        running,
        jnp.where(lane < 2 * heads, source, jnp.where(lane < 3 * heads, query, document)),
    )
    cols_ref[...] = cols
    rows_ref[...] = cols.T[: rows_ref.shape[0]]
    row = lax.broadcasted_iota(jnp.int32, (8, LANES), 0)
    table_ref[...] = jnp.where(row == 0, total, jnp.where(row == 1, last, first))


def factors_kernel(depth, device_ref, table_ref, factor_ref):
    stretches = table_ref.shape[0]
    device = device_ref[0]
    totals, lasts, firsts = table_ref[:, 0, :], table_ref[:, 1, :], table_ref[:, 2, :]
    stretch = lax.broadcasted_iota(jnp.int32, (stretches, LANES), 0) ^ device

    def at(values, index):
        return jnp.sum(jnp.where(stretch == index, values, 0.0), axis=0, keepdims=True)

    def span(low, high):
        inside = (stretch > low) & (stretch <= high)
        return jnp.exp(jnp.sum(jnp.where(inside, totals, 0.0), axis=0, keepdims=True))

    def reach(low_end, target):
        return jnp.where(at(firsts, target) == at(lasts, low_end), span(low_end, target - 1), 0.0)

    factors = []
    for distance in range(depth):
        low_end = ((device >> (distance + 1)) << (distance + 1)) + (1 << distance) - 1
        upper = ((device >> distance) & 1) == 1
        factors.append(jnp.where(upper, reach(low_end, device), 0.0))
    for distance in range(depth):
        low_end = ((device >> (distance + 1)) << (distance + 1)) + (1 << distance) - 1
        high_end = low_end + (1 << distance)
        factors.append(
            jnp.where(at(lasts, low_end) == at(lasts, high_end), span(low_end, high_end), 0.0)
        )
    middle = stretches // 2 - 1
    second = device // (stretches // 4) == 1
    for hop in (stretches // 4, stretches // 2):
        target = jnp.minimum(device + hop, stretches - 1)
        factors.append(jnp.where(second, reach(middle, target), 0.0))
    factor_ref[...] = jnp.zeros_like(factor_ref)
    for index, factor in enumerate(factors):
        factor_ref[index : index + 1, :] = factor


def states_kernel(heads, base, depth, q_ref, k_ref, v_ref, o_ref, cols_ref, level_ref, *outs):
    head = base + pl.program_id(0)
    cols = pltpu.roll(cols_ref[...], lax.rem(LANES - head, LANES), axis=1)
    source, query = cols[:, heads : heads + 1], cols[:, 2 * heads : 2 * heads + 1]
    outs[0][0] = dot(source * k_ref[...], v_ref[...], ((0,), (0,)))
    q, o = q_ref[...], o_ref[...]
    scaled = [(query * level_ref[:, d + 1 : d + 2]) * o for d in range(depth)]
    grads = dot(q, jnp.concatenate(scaled, axis=1), ((0,), (0,)))
    for d in range(depth):
        outs[d + 1][0] = grads[:, d * o.shape[1] : (d + 1) * o.shape[1]]


def local_kernel(
    heads, q_ref, k_ref, v_ref, o_ref, cols_ref, rows_ref, level_ref, gq_ref, gk_ref, gv_ref, out_ref
):
    head = pl.program_id(0)
    q, k, v, o = q_ref[...], k_ref[...], v_ref[...], o_ref[...]
    tokens = q.shape[0]
    cols = pltpu.roll(cols_ref[...], lax.rem(LANES - head, LANES), axis=1)
    document = cols_ref[:, 3 * heads : 3 * heads + 1]
    gap = cols[:, 0:1] - rows_ref[pl.ds(head, 1), :]
    visible = (
        lax.broadcasted_iota(jnp.int32, (tokens, tokens), 0) >= lane_of((tokens, tokens))
    ) & (document == rows_ref[3 * heads : 3 * heads + 1, :])
    within = jnp.where(visible, jnp.exp(jnp.minimum(gap, 0.0)), 0.0)
    scores = dot(q, k, ((1,), (1,)))
    grad_scores = dot(o, v, ((1,), (1,)))
    shared = within * grad_scores
    own = jnp.sum(shared * scores, axis=1, keepdims=True)
    level = level_ref[:, 0:1]
    shared = shared * level
    weighted = (within * level) * scores
    gv_ref[...] = dot(weighted, o, ((0,), (0,)))
    gq_ref[...] = dot(shared, k, ((1,), (0,)))
    gk_ref[...] = dot(shared, q, ((0,), (0,)))

    @pl.when(head == 0)
    def _():
        out_ref[...] = jnp.zeros_like(out_ref)

    out_ref[...] += jnp.where(lane_of(out_ref.shape) == 0, own, 0.0)


def levels_kernel(heads, base, levels, spare, last, *refs):
    q_ref, o_ref, cols_ref, level_ref, factor_ref, gq_in, lev_in = refs[:7]
    blocks = refs[7 : 7 + len(levels) + spare]
    gq_ref, lev_ref = refs[7 + len(levels) + spare :][:2]
    step = pl.program_id(0)
    head = base + step
    shift = lax.rem(LANES - head, LANES)
    query = pltpu.roll(cols_ref[...], shift, axis=1)[:, 2 * heads : 2 * heads + 1]
    factor = pltpu.roll(factor_ref[...], shift, axis=1)
    q, o = q_ref[...], o_ref[...]
    states = [block[0] for block in blocks[: len(levels)]]
    if spare:
        states[0] = states[0] + blocks[-1][0]
    width = o.shape[1]
    reached = dot(q, jnp.concatenate(states, axis=1), ((1,), (0,)))
    gq = gq_in[...]
    terms = jnp.zeros(lev_ref.shape, jnp.float32)
    for index, level in enumerate(levels):
        scale = query * factor[level - 1 : level, 0:1]
        gq = gq + (scale * level_ref[:, level : level + 1]) * dot(o, states[index], ((1,), (1,)))
        term = scale * jnp.sum(reached[:, index * width : (index + 1) * width] * o, axis=1, keepdims=True)
        terms = terms + jnp.where(lane_of(terms.shape) == level, term, 0.0)
    gq_ref[...] = gq

    @pl.when(step == 0)
    def _():
        lev_ref[...] = lev_in[...]

    lev_ref[...] += terms
    if last:
        turned_ref = refs[-1]

        @pl.when(step == pl.num_programs(0) - 1)
        def _():
            turned_ref[...] = lev_ref[...].T[: turned_ref.shape[0]]


def sources_kernel(heads, base, bit, block_row, refs_in, *refs):
    del refs_in
    device_ref, k_ref, v_ref, cols_ref, factor_ref, kept_ref, came_ref, gk_in, gv_in, gk_ref, gv_ref = refs
    head = base + pl.program_id(0)
    shift = lax.rem(LANES - head, LANES)
    source = pltpu.roll(cols_ref[...], shift, axis=1)[:, heads : heads + 1]
    factor = pltpu.roll(factor_ref[...], shift, axis=1)
    upper = ((device_ref[0] >> bit) & 1).astype(jnp.float32)
    own = upper + (1.0 - upper) * factor[block_row : block_row + 1, 0:1]
    state = own * kept_ref[0] + came_ref[0]
    gk_ref[...] = gk_in[...] + source * dot(v_ref[...], state, ((1,), (1,)))
    gv_ref[...] = gv_in[...] + source * dot(k_ref[...], state, ((1,), (0,)))


def blend_kernel(base, recipes, inputs, device_ref, factor_ref, *refs):
    arrays, outs = refs[:inputs], refs[inputs:]
    device = device_ref[0]
    factor = factor_ref[...]
    for head in range(arrays[0].shape[0]):
        column = factor[:, base + head : base + head + 1]
        values = [array[head] for array in arrays]
        for out, recipe in zip(outs, recipes):
            total = None
            for index, coefficient in recipe:
                term = values[index]
                weight = coefficient(device, lambda row: column[row : row + 1, :])
                term = term if weight is None else weight * term
                total = term if total is None else total + term
            out[head] = total


def blend(base, recipes, arrays, device, factor):
    shape = arrays[0].shape
    whole = pl.BlockSpec(memory_space=pltpu.VMEM)
    size = arrays[0].size * 4
    return pl.pallas_call(
        functools.partial(blend_kernel, base, recipes, len(arrays)),
        out_shape=[jax.ShapeDtypeStruct(shape, jnp.float32)] * len(recipes),
        in_specs=[pl.BlockSpec(memory_space=pltpu.SMEM), whole] + [whole] * len(arrays),
        out_specs=[whole] * len(recipes),
        compiler_params=pltpu.CompilerParams(vmem_limit_bytes=VMEM_LIMIT),
        cost_estimate=cost(size, size * (len(arrays) + len(recipes))),
    )(device, factor, *arrays)


def upper_or(bit, row):
    def weight(device, scalar):
        upper = ((device >> bit) & 1).astype(jnp.float32)
        return upper + (1.0 - upper) * scalar(row)

    return weight


def lower_or(bit, row):
    def weight(device, scalar):
        upper = ((device >> bit) & 1).astype(jnp.float32)
        return upper * scalar(row) + (1.0 - upper)

    return weight


def by(*rows):
    def weight(device, scalar):
        value = scalar(rows[0])
        for row in rows[1:]:
            value = value * scalar(row)
        return value

    return weight


def plain(device, scalar):
    return None


def send(array, route):
    return lax.ppermute(array, "seq", route)


def on_device(queries, key_input, value_input, grad_output, log_decay, level_weight, segment):
    stretches = lax.axis_size("seq")
    depth = stretches.bit_length() - 1
    tokens, heads = log_decay.shape
    width = queries.shape[1] // heads
    levels = level_weight.shape[1]
    quarter = stretches // 4
    device = lax.axis_index("seq").astype(jnp.int32).reshape(1)
    part_heads = heads // PARTS
    f32 = jnp.float32
    smem = pl.BlockSpec(memory_space=pltpu.SMEM)
    whole = pl.BlockSpec(memory_space=pltpu.VMEM)
    side_rows = -(-(3 * heads + 1) // 8) * 8
    factor_rows = -(-(2 * depth + 2) // 8) * 8
    token_bytes = tokens * width * 4
    state_bytes = width * width * 4
    pair_work = 2 * tokens * width * width * 3

    def shape(*dims):
        return jax.ShapeDtypeStruct(dims, f32)

    def head_block(base):
        return pl.BlockSpec((tokens, width), lambda i: (0, base + i))

    state_block = pl.BlockSpec((1, width, width), lambda i: (i, 0, 0))

    def fixed(*dims):
        return pl.BlockSpec(dims, lambda i: (0,) * len(dims))

    cols, rows, table = pl.pallas_call(
        functools.partial(prepare_kernel, heads),
        out_shape=[shape(tokens, LANES), shape(side_rows, tokens), shape(8, LANES)],
        in_specs=[whole, whole],
        out_specs=[whole] * 3,
        compiler_params=pltpu.CompilerParams(vmem_limit_bytes=VMEM_LIMIT),
    )(log_decay, segment.reshape(1, tokens))

    swaps = [[(i, i ^ (1 << d)) for i in range(stretches)] for d in range(depth)]
    table = table[None]
    for d in range(depth):
        table = jnp.concatenate([table, send(table, swaps[d])], axis=0)
    factor = pl.pallas_call(
        functools.partial(factors_kernel, depth),
        out_shape=shape(factor_rows, LANES),
        in_specs=[smem, whole],
        out_specs=whole,
        compiler_params=pltpu.CompilerParams(vmem_limit_bytes=VMEM_LIMIT),
    )(device, table)

    states, grads = [], []
    for part in range(PARTS):
        base = part * part_heads
        outs = pl.pallas_call(
            functools.partial(states_kernel, heads, base, depth),
            grid=(part_heads,),
            out_shape=[shape(part_heads, width, width)] * (depth + 1),
            in_specs=[head_block(base)] * 4 + [fixed(tokens, LANES), fixed(tokens, levels)],
            out_specs=[state_block] * (depth + 1),
            compiler_params=params(1),
            cost_estimate=cost(
                part_heads * pair_work * (depth + 1), part_heads * 4 * (token_bytes + state_bytes)
            ),
        )(queries, key_input, value_input, grad_output, cols, level_weight)
        states.append(outs[0])
        grads.append(outs[1:])

    def own_level(level):
        return level - 1

    def block_row(distance):
        return depth + distance

    third, fourth = 2 * depth, 2 * depth + 1
    up = [(i, i + quarter) for i in range(stretches) if not i // quarter & 1]
    down = [(i + quarter, i) for i in range(stretches) if not i // quarter & 1]
    second_third = [(quarter + i, 2 * quarter + i) for i in range(quarter)]
    second_fourth = [(quarter + i, 3 * quarter + i) for i in range(quarter)]
    third_second = [(b, a) for a, b in second_third]
    fourth_second = [(b, a) for a, b in second_fourth]

    came = [[None] * (depth + 1) for _ in range(PARTS)]
    spare = [None] * PARTS
    kept, sources = [None] * PARTS, [None] * PARTS
    running = list(states)
    parts = range(PARTS)
    from_third = [send(grads[p][depth - 1], third_second) for p in parts]
    for d in range(depth - 2):
        for p in parts:
            came[p][d + 1] = send(running[p], swaps[d])
        for p in parts:
            recipe = [(0, upper_or(d, block_row(d))), (1, lower_or(d, block_row(d)))]
            (running[p],) = blend(
                p * part_heads, [recipe], [running[p], came[p][d + 1]], device, factor
            )
    from_fourth = [send(grads[p][depth - 1], fourth_second) for p in parts]
    for p in parts:
        came[p][depth - 1] = send(running[p], up)
        spare[p] = send(running[p], second_fourth)
    from_upper = [None] * PARTS
    for p in parts:
        recipe = [
            (0, by(own_level(depth - 1))),
            (1, by(block_row(depth - 2), third)),
        ]
        (message,) = blend(
            p * part_heads, [recipe], [grads[p][depth - 2], from_third[p]], device, factor
        )
        from_upper[p] = send(message, down)
    for p in parts:
        recipe = [(0, plain), (1, by(block_row(depth - 2)))]
        (half,) = blend(
            p * part_heads, [recipe], [running[p], came[p][depth - 1]], device, factor
        )
        came[p][depth] = send(half, second_third)
    for p in parts:
        pending, source_arrays = None, [from_upper[p], from_third[p], from_fourth[p]]
        total = [(0, plain), (1, by(third)), (2, by(fourth))]
        if depth == 2:
            (kept[p],) = blend(p * part_heads, [total], source_arrays, device, factor)
            continue
        (pending,) = blend(p * part_heads, [total], source_arrays, device, factor)
        for d in range(depth - 3, -1, -1):
            message = [(0, lower_or(d, block_row(d))), (1, by(own_level(d + 1)))]
            (outgoing,) = blend(p * part_heads, [message], [pending, grads[p][d]], device, factor)
            arrived = send(outgoing, swaps[d])
            if d == 0:
                kept[p], sources[p] = pending, arrived
            else:
                recipe = [(0, upper_or(d, block_row(d))), (1, plain)]
                (pending,) = blend(p * part_heads, [recipe], [pending, arrived], device, factor)

    grad_query, grad_key, grad_value, terms = pl.pallas_call(
        functools.partial(local_kernel, heads),
        grid=(heads,),
        out_shape=[shape(*queries.shape)] * 3 + [shape(tokens, LANES)],
        in_specs=[head_block(0)] * 4
        + [fixed(tokens, LANES), fixed(side_rows, tokens), fixed(tokens, levels)],
        out_specs=[head_block(0)] * 3 + [fixed(tokens, LANES)],
        compiler_params=params(1),
        cost_estimate=cost(heads * 30 * tokens * tokens * width, heads * 7 * token_bytes),
    )(queries, key_input, value_input, grad_output, cols, rows, level_weight)

    turned_rows = -(-levels // 8) * 8

    def add_levels(chosen, part, grad_query, terms, last):
        blocks = [came[part][level] for level in chosen]
        extra = chosen == [depth]
        if extra:
            blocks.append(spare[part])
        base = part * part_heads
        outs = pl.pallas_call(
            functools.partial(levels_kernel, heads, base, chosen, int(extra), last),
            grid=(part_heads,),
            out_shape=[shape(*queries.shape), shape(tokens, LANES)]
            + [shape(turned_rows, tokens)] * last,
            in_specs=[head_block(base)] * 2
            + [fixed(tokens, LANES), fixed(tokens, levels), fixed(factor_rows, LANES)]
            + [head_block(base), fixed(tokens, LANES)]
            + [state_block] * len(blocks),
            out_specs=[head_block(base), fixed(tokens, LANES)]
            + [fixed(turned_rows, tokens)] * last,
            input_output_aliases={5: 0, 6: 1},
            compiler_params=params(1),
            cost_estimate=cost(
                part_heads * pair_work * 2 * len(chosen), part_heads * 4 * token_bytes
            ),
        )(queries, grad_output, cols, level_weight, factor, grad_query, terms, *blocks)
        return outs

    for p in parts:
        grad_query, terms = add_levels(list(range(1, depth)), p, grad_query, terms, False)
    for p in parts:
        last = p == PARTS - 1
        outs = add_levels([depth], p, grad_query, terms, last)
        grad_query, terms = outs[:2]
        if last:
            turned = outs[2]

    groups = lax.axis_size("head")
    others = [
        lax.ppermute(turned, "head", [(i, (i + k) % groups) for i in range(groups)])
        for k in range(1, groups)
    ]

    for p in parts:
        base = p * part_heads
        grad_key, grad_value = pl.pallas_call(
            functools.partial(sources_kernel, heads, base, 0, block_row(0), None),
            grid=(part_heads,),
            out_shape=[shape(*queries.shape)] * 2,
            in_specs=[smem, head_block(base), head_block(base), fixed(tokens, LANES)]
            + [fixed(factor_rows, LANES), state_block, state_block]
            + [head_block(base)] * 2,
            out_specs=[head_block(base)] * 2,
            input_output_aliases={7: 0, 8: 1},
            compiler_params=params(1),
            cost_estimate=cost(part_heads * pair_work * 2, part_heads * 6 * token_bytes),
        )(device, key_input, value_input, cols, factor, kept[p], sources[p], grad_key, grad_value)

    def level_sum_kernel(*refs):
        total = refs[0][...]
        for ref in refs[1:-1]:
            total = total + ref[...]
        wide = jnp.concatenate(
            [total, jnp.zeros((LANES - turned_rows, tokens), f32)], axis=0
        )
        refs[-1][...] = wide.T[:, :levels]

    grad_level = pl.pallas_call(
        level_sum_kernel,
        out_shape=shape(tokens, levels),
        in_specs=[whole] * groups,
        out_specs=whole,
    )(turned, *others)
    return grad_query, grad_key, grad_value, grad_level


def solution(mesh):
    in_specs = (
        P("seq", "head"),
        P("seq", "head"),
        P("seq", "head"),
        P("seq", "head"),
        P("seq", "head"),
        P("seq", None),
        P("seq"),
    )
    out_specs = (P("seq", "head"), P("seq", "head"), P("seq", "head"), P("seq", None))
    return jax.shard_map(
        on_device, mesh=mesh, in_specs=in_specs, out_specs=out_specs, check_vma=False
    )
```

```python
import functools

import jax
import jax.numpy as jnp
from jax import lax
from jax.experimental import pallas as pl
from jax.experimental.pallas import tpu as pltpu
from jax.sharding import PartitionSpec as P

HIGH = lax.Precision.HIGH
EXACT = lax.Precision.HIGHEST
LANES = 128
PARTS = 2
VMEM_LIMIT = 6 * 1024 * 1024
WHOLE = pl.BlockSpec(memory_space=pltpu.VMEM)
SCALARS = pl.BlockSpec(memory_space=pltpu.SMEM)
FAR = pl.BlockSpec(memory_space=pltpu.HBM)
ANYWHERE = pl.BlockSpec(memory_space=pl.ANY)
ROWS, COLS = ((1,), (0,)), ((0,), (0,))
TURNED = ((1,), (1,))


def dot(a, b, over, precision=HIGH):
    return lax.dot_general(
        a, b, (over, ((), ())), precision=precision, preferred_element_type=jnp.float32
    )


def params(steps=0):
    return pltpu.CompilerParams(
        dimension_semantics=("arbitrary",) * steps or None, vmem_limit_bytes=VMEM_LIMIT
    )


def cost(flops, moved):
    return pl.CostEstimate(flops=int(flops), bytes_accessed=int(moved), transcendentals=0)


def iota(shape, axis):
    return lax.broadcasted_iota(jnp.int32, shape, axis)


def near(array):
    return pltpu.with_memory_space_constraint(array, pltpu.VMEM)


def far(array):
    return pltpu.with_memory_space_constraint(array, pltpu.HBM)


def upright(row, width):
    return jnp.broadcast_to(row, (width, row.shape[1])).T


def ship(source, target, from_columns, to_columns, sem):
    copy = pltpu.make_async_copy(
        source.at[:, pl.ds(from_columns.start, from_columns.stop - from_columns.start)],
        target.at[:, pl.ds(to_columns.start, to_columns.stop - to_columns.start)],
        sem,
    )
    copy.start()
    return copy


def join_kernel(own_ref, came_ref, out_ref):
    half = own_ref.shape[0]
    out_ref[:half] = own_ref[...]
    out_ref[half:] = came_ref[...]


def total_kernel(*refs):
    total = refs[0][...]
    for ref in refs[1:-1]:
        total = total + ref[...]
    refs[-1][...] = total[: refs[-1].shape[0]]


def prepare_kernel(
    heads, device_ref, decay_hbm, segment_hbm, cols_ref, rows_ref, source_ref, query_ref, table_ref,
    decay_ref, segment_ref, sems,
):
    del device_ref
    tokens = segment_ref.shape[1]
    copies = [
        pltpu.make_async_copy(decay_hbm, decay_ref, sems.at[0]),
        pltpu.make_async_copy(segment_hbm, segment_ref, sems.at[1]),
    ]
    for copy in copies:
        copy.start()
    for copy in copies:
        copy.wait()
    sooner = iota((tokens, tokens), 0) <= iota((tokens, tokens), 1)
    running = dot(decay_ref[...], sooner.astype(jnp.float32), ROWS, EXACT)
    document = segment_ref[...].astype(jnp.float32)
    total, first, last = running[:, tokens - 1 :], document[:, :1], document[:, tokens - 1 :]
    source_ref[...] = jnp.exp(total - running) * (document == last).astype(jnp.float32)
    query_ref[...] = jnp.exp(running) * (document == first).astype(jnp.float32)
    spare = LANES - heads - 1
    rows = jnp.concatenate([running, document, jnp.zeros((spare, tokens), jnp.float32)], axis=0)
    rows_ref[...] = rows[: rows_ref.shape[0]]
    cols = rows.T
    cols_ref[...] = cols
    row = iota((8, LANES), 0)
    table_ref[0] = jnp.where(row == 0, cols[tokens - 1 :], jnp.where(row == 1, last, first))


def first_kernel(heads, source_ref, k_ref, v_ref, wk_ref, wv_ref, *states):
    width = k_ref.shape[1] // heads
    part_heads = states[0].shape[0]
    for head in range(heads):
        at = slice(head * width, (head + 1) * width)
        weight = upright(source_ref[head : head + 1, :], width)
        weighted = weight * k_ref[:, at]
        v = v_ref[:, at]
        wk_ref[:, at] = weighted
        wv_ref[:, at] = weight * v
        states[head // part_heads][head % part_heads] = dot(weighted, v, COLS)


def second_kernel(
    heads, depth, level_ref, query_ref, q_ref, o_ref, after_ref, uo_ref, spread_ref, *outs
):
    del after_ref
    width = q_ref.shape[1] // heads
    for d in range(depth):
        spread_ref[d] = upright(level_ref[d + 1 : d + 2, :], width)
    part_heads = outs[0].shape[0]
    for head in range(heads):
        at = slice(head * width, (head + 1) * width)
        weight = upright(query_ref[head : head + 1, :], width)
        weighted = weight * o_ref[:, at]
        uo_ref[:, at] = weighted
        scaled = jnp.concatenate([spread_ref[d] * weighted for d in range(depth)], axis=1)
        grads = dot(q_ref[:, at], scaled, COLS)
        part, place = divmod(head, part_heads)
        for d in range(depth):
            outs[part * depth + d][place] = grads[:, d * width : (d + 1) * width]


def local_kernel(
    heads, base, q_ref, k_ref, v_ref, o_ref, cols_ref, rows_ref, level_ref, *refs
):
    terms_in = refs[0] if base else None
    gq_ref, gk_ref, gv_ref, terms_ref, shown_ref, total_ref = refs[-6:]
    tokens = rows_ref.shape[1]
    width = k_ref.shape[1] // heads
    shown = (iota((tokens, tokens), 0) <= iota((tokens, tokens), 1)) & (
        cols_ref[:, heads : heads + 1] == rows_ref[heads : heads + 1, :]
    )
    shown_ref[...] = jnp.where(shown, 0.0, -jnp.inf)
    total_ref[...] = jnp.zeros_like(total_ref)
    level = level_ref[0:1, :]
    for place in range(gq_ref.shape[1] // width):
        head = base + place
        at = slice(head * width, (head + 1) * width)
        to = slice(place * width, (place + 1) * width)
        q, k, v, o = q_ref[:, at], k_ref[:, at], v_ref[:, at], o_ref[:, at]
        gap = rows_ref[head : head + 1, :] - cols_ref[:, head : head + 1]
        within = jnp.exp(jnp.minimum(gap, shown_ref[...]))
        scores = dot(k, q, TURNED)
        shared = within * dot(v, o, TURNED)
        total_ref[...] += jnp.sum((shared * scores).reshape(tokens // 8, 8, tokens), axis=0)
        shared = shared * level
        gv_ref[:, to] = dot((within * level) * scores, o, ROWS)
        gk_ref[:, to] = dot(shared, q, ROWS)
        gq_ref[:, to] = dot(shared, k, COLS)
    own = jnp.sum(total_ref[...], axis=0, keepdims=True)
    terms = jnp.where(iota(terms_ref.shape, 0) == 0, own, 0.0)
    terms_ref[...] = terms if terms_in is None else terms + terms_in[...]


def factors_kernel(depth, device_ref, table_ref, factor_ref):
    stretches = table_ref.shape[0]
    device = device_ref[0]
    totals, lasts, firsts = table_ref[:, 0, :], table_ref[:, 1, :], table_ref[:, 2, :]
    stretch = iota((stretches, LANES), 0) ^ device

    def at(values, index):
        return jnp.sum(jnp.where(stretch == index, values, 0.0), axis=0, keepdims=True)

    def span(low, high):
        inside = (stretch > low) & (stretch <= high)
        return jnp.exp(jnp.sum(jnp.where(inside, totals, 0.0), axis=0, keepdims=True))

    def reach(low_end, target):
        return jnp.where(at(firsts, target) == at(lasts, low_end), span(low_end, target - 1), 0.0)

    factors = []
    for distance in range(depth):
        low_end = ((device >> (distance + 1)) << (distance + 1)) + (1 << distance) - 1
        upper = ((device >> distance) & 1) == 1
        factors.append(jnp.where(upper, reach(low_end, device), 0.0))
    for distance in range(depth):
        low_end = ((device >> (distance + 1)) << (distance + 1)) + (1 << distance) - 1
        high_end = low_end + (1 << distance)
        factors.append(
            jnp.where(at(lasts, low_end) == at(lasts, high_end), span(low_end, high_end), 0.0)
        )
    middle = stretches // 2 - 1
    second = device // (stretches // 4) == 1
    for hop in (stretches // 4, stretches // 2):
        target = jnp.minimum(device + hop, stretches - 1)
        factors.append(jnp.where(second, reach(middle, target), 0.0))
    factor_ref[...] = jnp.zeros_like(factor_ref)
    for index, factor in enumerate(factors):
        factor_ref[index : index + 1, :] = factor


def levels_kernel(heads, base, chosen, spare, out_at, device_ref, *refs):
    q_ref, uo_ref, spread_ref, factor_ref, gq_in, terms_in = refs[:6]
    blocks = refs[6 : 6 + len(chosen) + spare]
    if out_at is None:
        gq_ref, terms_ref, *totals = refs[-(2 + len(chosen)) :]
    else:
        gq_hbm, terms_ref, *totals, gq_ref, sems = refs[-(4 + len(chosen)) :]
    copies = []
    width = spread_ref.shape[2]
    device = device_ref[0]
    for place in range(gq_in.shape[1] // width):
        head = base + place
        at = slice(head * width, (head + 1) * width)
        to = slice(place * width, (place + 1) * width)
        states = [block[place] for block in blocks[: len(chosen)]]
        if spare:
            fourth = device & (1 << (chosen[0] - 2)) != 0
            states[0] = jnp.where(fourth, blocks[-1][place], states[0])
        states = [
            factor_ref[level - 1 : level, head : head + 1] * state
            for level, state in zip(chosen, states)
        ]
        q, uo = q_ref[:, at], uo_ref[:, at]
        reached = dot(q, jnp.concatenate(states, axis=1), ROWS)
        back = dot(uo, jnp.concatenate(states, axis=0), TURNED)
        gq = gq_in[:, to]
        for index, level in enumerate(chosen):
            here = slice(index * width, (index + 1) * width)
            gq = gq + spread_ref[level - 1] * back[:, here]
            term = reached[:, here] * uo
            totals[index][...] = term if place == 0 else totals[index][...] + term
        gq_ref[:, to] = gq
        if out_at is not None:
            copies.append(ship(gq_ref, gq_hbm, to, at, sems.at[place]))
    terms = terms_in[...]
    for total, level in zip(totals, chosen):
        row = jnp.sum(total[...].T, axis=0, keepdims=True)
        terms = terms + jnp.where(iota(terms.shape, 0) == level, row, 0.0)
    terms_ref[...] = terms
    for copy in copies:
        copy.wait()


def sources_kernel(heads, base, row, device_ref, wk_ref, wv_ref, factor_ref, kept_ref, came_ref, *refs):
    gk_in, gv_in = refs[:2]
    gk_hbm, gv_hbm, gk_ref, gv_ref, sems = refs[-5:]
    copies = []
    width = kept_ref.shape[2]
    upper = (device_ref[0] & 1).astype(jnp.float32)
    for place in range(kept_ref.shape[0]):
        head = base + place
        at = slice(head * width, (head + 1) * width)
        to = slice(place * width, (place + 1) * width)
        own = upper + (1.0 - upper) * factor_ref[row : row + 1, head : head + 1]
        state = own * kept_ref[place] + came_ref[place]
        gk_ref[:, to] = gk_in[:, to] + dot(wv_ref[:, at], state, TURNED)
        copies.append(ship(gk_ref, gk_hbm, to, at, sems.at[0, place]))
        gv_ref[:, to] = gv_in[:, to] + dot(wk_ref[:, at], state, ROWS)
        copies.append(ship(gv_ref, gv_hbm, to, at, sems.at[1, place]))
    for copy in copies:
        copy.wait()


def blend_kernel(base, recipes, inputs, after, device_ref, factor_ref, *refs):
    arrays, outs = refs[:inputs], refs[inputs + after :]
    device = device_ref[0]
    factor = factor_ref[...]
    for head in range(arrays[0].shape[0]):
        column = factor[:, base + head : base + head + 1]
        for out, recipe in zip(outs, recipes):
            total = None
            for index, coefficient in recipe:
                weight = coefficient(device, lambda row: column[row : row + 1, :])
                term = arrays[index][head]
                term = term if weight is None else weight * term
                total = term if total is None else total + term
            out[head] = total


def blend(base, recipes, arrays, device, factor, after=()):
    size = arrays[0].size * 4
    return pl.pallas_call(
        functools.partial(blend_kernel, base, recipes, len(arrays), len(after)),
        out_shape=[jax.ShapeDtypeStruct(arrays[0].shape, jnp.float32)] * len(recipes),
        in_specs=[SCALARS, WHOLE] + [WHOLE] * len(arrays) + [ANYWHERE] * len(after),
        out_specs=[WHOLE] * len(recipes),
        compiler_params=params(),
        cost_estimate=cost(size, size * (len(arrays) + len(recipes))),
    )(device, *map(near, (factor, *arrays)), *after)


def upper_flag(device, bit):
    return ((device >> bit) & 1).astype(jnp.float32)


def upper_or(bit, row):
    return lambda device, scalar: upper_flag(device, bit) * (1.0 - scalar(row)) + scalar(row)


def lower_or(bit, row):
    return lambda device, scalar: upper_flag(device, bit) * (scalar(row) - 1.0) + 1.0


def lower(bit):
    return lambda device, scalar: 1.0 - upper_flag(device, bit)


def by(row):
    return lambda device, scalar: scalar(row)


def both(row, other):
    return lambda device, scalar: scalar(row) * scalar(other)


def plain(device, scalar):
    return None


def send(array, route):
    return lax.ppermute(array, "seq", route)


def on_device(queries, key_input, value_input, grad_output, log_decay, level_weight, segment):
    stretches = lax.axis_size("seq")
    depth = stretches.bit_length() - 1
    tokens, heads = log_decay.shape
    width = queries.shape[1] // heads
    levels = level_weight.shape[1]
    quarter = stretches // 4
    device = lax.axis_index("seq").astype(jnp.int32).reshape(1)
    part_heads = heads // PARTS
    parts = range(PARTS)
    part_width = part_heads * width
    factor_rows = -(-(2 * depth + 2) // 8) * 8
    side_rows = -(-(heads + 1) // 8) * 8
    turned_rows = -(-levels // 8) * 8
    token_bytes = tokens * width * 4
    work = 6 * tokens * width * width

    def shape(*dims):
        return jax.ShapeDtypeStruct(dims, jnp.float32)

    tall = shape(tokens, heads * width)
    state = shape(part_heads, width, width)
    decay_rows, level_rows = log_decay.T, level_weight.T

    near_k, near_v, near_q, near_o = key_input, value_input, queries, grad_output
    cols, rows, source, query, table = pl.pallas_call(
        functools.partial(prepare_kernel, heads),
        out_shape=[shape(tokens, LANES), shape(side_rows, tokens)]
        + [shape(heads, tokens)] * 2
        + [shape(1, 8, LANES)],
        in_specs=[SCALARS, FAR, FAR],
        out_specs=[WHOLE] * 5,
        scratch_shapes=[
            pltpu.VMEM((heads, tokens), jnp.float32),
            pltpu.VMEM((1, tokens), jnp.int32),
            pltpu.SemaphoreType.DMA((2,)),
        ],
        compiler_params=params(),
    )(device, far(decay_rows), far(segment.reshape(1, tokens)))

    weighted_k, weighted_v, *states = pl.pallas_call(
        functools.partial(first_kernel, heads),
        out_shape=[tall] * 2 + [state] * PARTS,
        in_specs=[WHOLE] * 3,
        out_specs=[WHOLE] * (2 + PARTS),
        compiler_params=params(),
        cost_estimate=cost(heads * work, heads * 2 * token_bytes),
    )(*map(near, (source, near_k, near_v)))

    swaps = [[(i, i ^ (1 << d)) for i in range(stretches)] for d in range(depth)]
    tables = [table]
    for d in range(depth):
        table = pl.pallas_call(
            join_kernel,
            out_shape=shape(2 << d, 8, LANES),
            in_specs=[WHOLE] * 2,
            out_specs=WHOLE,
            compiler_params=params(),
        )(near(table), near(send(table, swaps[d])))
        tables.append(table)

    weighted_o, spread, *grads = pl.pallas_call(
        functools.partial(second_kernel, heads, depth),
        out_shape=[tall, shape(depth, tokens, width)] + [state] * (PARTS * depth),
        in_specs=[WHOLE] * 4 + [ANYWHERE],
        out_specs=[WHOLE] * (2 + PARTS * depth),
        compiler_params=params(),
        cost_estimate=cost(heads * depth * work, heads * 2 * token_bytes),
    )(level_rows, *map(near, (query, near_q, near_o)), tables[1])
    grads = [grads[p * depth : (p + 1) * depth] for p in parts]

    factor = pl.pallas_call(
        functools.partial(factors_kernel, depth),
        out_shape=shape(factor_rows, LANES),
        in_specs=[SCALARS, WHOLE],
        out_specs=WHOLE,
        compiler_params=params(),
    )(device, near(table))

    def own_level(level):
        return level - 1

    def block_row(distance):
        return depth + distance

    third, fourth = 2 * depth, 2 * depth + 1
    second_third = [(quarter + i, 2 * quarter + i) for i in range(quarter)]
    second_fourth = [(quarter + i, 3 * quarter + i) for i in range(quarter)]
    third_second = [(b, a) for a, b in second_third]
    fourth_second = [(b, a) for a, b in second_fourth]

    gq, gk, gv = ([None] * PARTS for _ in range(3))
    terms = None
    shown_terms = [None] * PARTS
    for p in parts:
        before = [] if terms is None else [near(terms)]
        gq[p], gk[p], gv[p], terms = pl.pallas_call(
            functools.partial(local_kernel, heads, p * part_heads),
            out_shape=[shape(tokens, part_width)] * 3 + [shape(turned_rows, tokens)],
            in_specs=[WHOLE] * (7 + len(before)),
            out_specs=[WHOLE] * 4,
            scratch_shapes=[
                pltpu.VMEM((tokens, tokens), jnp.float32),
                pltpu.VMEM((8, tokens), jnp.float32),
            ],
            compiler_params=params(),
            cost_estimate=cost(part_heads * 30 * tokens * tokens * width, 0),
        )(*map(near, (near_q, near_k, near_v, near_o, cols, rows)), level_rows, *before)
        shown_terms[p] = terms

    def add_levels(chosen, p, gq, terms, blocks, out=None, final=False):
        in_hbm = [] if out is None else [out]
        inputs = 7 + len(blocks)
        scratch = [pltpu.VMEM((tokens, width), jnp.float32)] * len(chosen)
        if final:
            scratch += [
                pltpu.VMEM((tokens, part_width), jnp.float32),
                pltpu.SemaphoreType.DMA((part_heads,)),
            ]
        return pl.pallas_call(
            functools.partial(
                levels_kernel,
                heads,
                p * part_heads,
                chosen,
                len(blocks) - len(chosen),
                p if final else None,
            ),
            out_shape=[
                shape(tokens, heads * width if final else part_width),
                shape(turned_rows, tokens),
            ],
            in_specs=[SCALARS] + [WHOLE] * (inputs - 1) + [FAR] * len(in_hbm),
            out_specs=[FAR if final else WHOLE, WHOLE],
            scratch_shapes=scratch,
            input_output_aliases={inputs: 0} if in_hbm else {},
            compiler_params=params(),
            cost_estimate=cost(part_heads * work * 2 * len(chosen), 0),
        )(device, *map(near, (near_q, weighted_o, spread, factor, gq, terms, *blocks)), *in_hbm)

    came = [[None] * (depth + 1) for _ in parts]
    running = list(states)
    from_third = [send(grads[p][depth - 1], third_second) for p in parts]
    from_fourth = [send(grads[p][depth - 1], fourth_second) for p in parts]
    for d in range(depth - 2):
        for p in parts:
            came[p][d + 1] = send(running[p], swaps[d])
        for p in parts:
            recipe = [(0, upper_or(d, block_row(d))), (1, lower_or(d, block_row(d)))]
            arrays = [running[p], came[p][d + 1]]
            (running[p],) = blend(
                p * part_heads, [recipe], arrays, device, factor
            )
    spare, crossed = [None] * PARTS, [None] * PARTS
    for p in parts:
        recipe = [
            (0, lower(depth - 2)),
            (1, by(own_level(depth - 1))),
            (2, both(block_row(depth - 2), third)),
        ]
        arrays = [running[p], grads[p][depth - 2], from_third[p]]
        (message,) = blend(p * part_heads, [recipe], arrays, device, factor)
        crossed[p] = send(message, swaps[depth - 2])
        spare[p] = send(running[p], second_fourth)
        came[p][depth - 1] = crossed[p]
    if depth > 2:
        chosen = list(range(1, depth - 1))
        for p in parts:
            blocks = [came[p][level] for level in chosen]
            gq[p], terms = add_levels(chosen, p, gq[p], terms, blocks)
    kept, sources = [None] * PARTS, [None] * PARTS
    for p in parts:
        recipe = [(0, plain), (1, by(block_row(depth - 2)))]
        (half,) = blend(
            p * part_heads, [recipe], [running[p], crossed[p]], device, factor, [terms]
        )
        came[p][depth] = send(half, second_third)
    for p in parts:
        total = [(0, lower(depth - 2)), (1, by(third)), (2, by(fourth))]
        arrays = [crossed[p], from_third[p], from_fourth[p]]
        (pending,) = blend(p * part_heads, [total], arrays, device, factor)
        for d in range(depth - 3, -1, -1):
            message = [(0, lower_or(d, block_row(d))), (1, by(own_level(d + 1)))]
            (outgoing,) = blend(p * part_heads, [message], [pending, grads[p][d]], device, factor)
            arrived = send(outgoing, swaps[d])
            if d > 0:
                recipe = [(0, upper_or(d, block_row(d))), (1, plain)]
                (pending,) = blend(p * part_heads, [recipe], [pending, arrived], device, factor)
        kept[p], sources[p] = pending, arrived
    for p in parts:
        gq[p], terms = add_levels([depth - 1], p, gq[p], terms, [crossed[p]])
    grad_query = None
    for p in parts:
        blocks = [came[p][depth], spare[p]]
        grad_query, terms = add_levels([depth], p, gq[p], terms, blocks, grad_query, True)
    groups = lax.axis_size("head")
    others = [
        lax.ppermute(terms, "head", [(i, (i + k) % groups) for i in range(groups)])
        for k in range(1, groups)
    ]
    done = []
    for p in parts:
        done = pl.pallas_call(
            functools.partial(sources_kernel, heads, p * part_heads, block_row(0)),
            out_shape=[tall] * 2,
            in_specs=[SCALARS] + [WHOLE] * 7 + [FAR] * len(done),
            out_specs=[FAR] * 2,
            scratch_shapes=[pltpu.VMEM((tokens, part_width), jnp.float32)] * 2
            + [pltpu.SemaphoreType.DMA((2, part_heads))],
            input_output_aliases={8: 0, 9: 1} if done else {},
            compiler_params=params(),
            cost_estimate=cost(part_heads * work * 2, 0),
        )(
            device,
            *map(near, (weighted_k, weighted_v, factor, kept[p], sources[p], gk[p], gv[p])),
            *done,
        )
    grad_level = pl.pallas_call(
        total_kernel,
        out_shape=shape(levels, tokens),
        in_specs=[WHOLE] * groups,
        out_specs=WHOLE,
        compiler_params=params(),
    )(terms, *others)
    return grad_query, done[0], done[1], grad_level.T


def solution(mesh):
    in_specs = (
        P("seq", "head"),
        P("seq", "head"),
        P("seq", "head"),
        P("seq", "head"),
        P("seq", "head"),
        P("seq", None),
        P("seq"),
    )
    out_specs = (P("seq", "head"), P("seq", "head"), P("seq", "head"), P("seq", None))
    return jax.shard_map(
        on_device, mesh=mesh, in_specs=in_specs, out_specs=out_specs, check_vma=False
    )
```

```python
import functools

import jax
import jax.numpy as jnp
from jax import lax
from jax.experimental import pallas as pl
from jax.experimental.pallas import tpu as pltpu
from jax.sharding import PartitionSpec as P

HIGH = lax.Precision.HIGH
EXACT = lax.Precision.HIGHEST
LANES = 128
PARTS = 2
VMEM_LIMIT = 6 * 1024 * 1024
WHOLE = pl.BlockSpec(memory_space=pltpu.VMEM)
SCALARS = pl.BlockSpec(memory_space=pltpu.SMEM)
FAR = pl.BlockSpec(memory_space=pltpu.HBM)
ANYWHERE = pl.BlockSpec(memory_space=pl.ANY)
ROWS, COLS = ((1,), (0,)), ((0,), (0,))
TURNED = ((1,), (1,))


def dot(a, b, over, precision=HIGH):
    return lax.dot_general(
        a, b, (over, ((), ())), precision=precision, preferred_element_type=jnp.float32
    )


def params(steps=0):
    return pltpu.CompilerParams(
        dimension_semantics=("arbitrary",) * steps or None, vmem_limit_bytes=VMEM_LIMIT
    )


def cost(flops, moved):
    return pl.CostEstimate(flops=1, bytes_accessed=1, transcendentals=0)


def iota(shape, axis):
    return lax.broadcasted_iota(jnp.int32, shape, axis)


def near(array):
    return pltpu.with_memory_space_constraint(array, pltpu.VMEM)


def far(array):
    return pltpu.with_memory_space_constraint(array, pltpu.HBM)


def upright(row, width):
    return jnp.broadcast_to(row, (width, row.shape[1])).T


def ship(source, target, from_columns, to_columns, sem):
    copy = pltpu.make_async_copy(
        source.at[:, pl.ds(from_columns.start, from_columns.stop - from_columns.start)],
        target.at[:, pl.ds(to_columns.start, to_columns.stop - to_columns.start)],
        sem,
    )
    copy.start()
    return copy


def join_kernel(own_ref, came_ref, after_ref, out_ref):
    del after_ref
    half = own_ref.shape[0]
    out_ref[:half] = own_ref[...]
    out_ref[half:] = came_ref[...]


def total_kernel(*refs):
    total = refs[0][...]
    for ref in refs[1:-1]:
        total = total + ref[...]
    refs[-1][...] = total[: refs[-1].shape[0]]


def first_kernel(
    heads, device_ref, decay_hbm, segment_hbm, k_hbm, v_hbm, q_hbm, o_hbm, k_ref, v_ref, q_ref,
    o_ref, cols_ref, rows_ref, source_ref, query_ref, table_ref, decay_ref, segment_ref, sems,
):
    del device_ref
    tokens = segment_ref.shape[1]
    pairs = (
        (decay_hbm, decay_ref), (segment_hbm, segment_ref), (k_hbm, k_ref), (v_hbm, v_ref),
        (q_hbm, q_ref), (o_hbm, o_ref),
    )
    copies = [
        pltpu.make_async_copy(source, target, sems.at[index])
        for index, (source, target) in enumerate(pairs)
    ]
    for copy in copies:
        copy.start()
    copies[0].wait()
    copies[1].wait()
    sooner = iota((tokens, tokens), 0) <= iota((tokens, tokens), 1)
    running = dot(decay_ref[...], sooner.astype(jnp.float32), ROWS, EXACT)
    document = segment_ref[...].astype(jnp.float32)
    total, first, last = running[:, tokens - 1 :], document[:, :1], document[:, tokens - 1 :]
    source_ref[...] = jnp.exp(total - running) * (document == last).astype(jnp.float32)
    query_ref[...] = jnp.exp(running) * (document == first).astype(jnp.float32)
    spare = LANES - heads - 1
    rows = jnp.concatenate([running, document, jnp.zeros((spare, tokens), jnp.float32)], axis=0)
    rows_ref[...] = rows[: rows_ref.shape[0]]
    cols = rows.T
    cols_ref[...] = cols
    row = iota((8, LANES), 0)
    table_ref[0] = jnp.where(row == 0, cols[tokens - 1 :], jnp.where(row == 1, last, first))
    for copy in copies[2:]:
        copy.wait()


def states_kernel(heads, source_ref, k_ref, v_ref, after_ref, wk_ref, wv_ref, *states):
    del after_ref
    width = k_ref.shape[1] // heads
    for head in range(heads):
        at = slice(head * width, (head + 1) * width)
        weight = upright(source_ref[head : head + 1, :], width)
        weighted = weight * k_ref[:, at]
        v = v_ref[:, at]
        wk_ref[:, at] = weighted
        wv_ref[:, at] = weight * v
        part, place = divmod(head, states[0].shape[0])
        states[part][place] = dot(weighted, v, COLS)


def second_kernel(
    heads, depth, level_ref, query_ref, q_ref, o_ref, uo_ref, spread_ref, *outs
):
    width = q_ref.shape[1] // heads
    for d in range(depth):
        spread_ref[d] = upright(level_ref[d + 1 : d + 2, :], width)
    for head in range(heads):
        at = slice(head * width, (head + 1) * width)
        weight = upright(query_ref[head : head + 1, :], width)
        weighted = weight * o_ref[:, at]
        uo_ref[:, at] = weighted
        scaled = jnp.concatenate([spread_ref[d] * weighted for d in range(depth)], axis=1)
        grads = dot(q_ref[:, at], scaled, COLS)
        part, place = divmod(head, outs[0].shape[0])
        for d in range(depth):
            outs[part * depth + d][place] = grads[:, d * width : (d + 1) * width]


def local_kernel(
    heads, base, q_ref, k_ref, v_ref, o_ref, cols_ref, rows_ref, level_ref, *refs
):
    terms_in = refs[0] if base else None
    gq_ref, gk_ref, gv_ref, terms_ref, shown_ref, total_ref = refs[-6:]
    tokens = rows_ref.shape[1]
    width = k_ref.shape[1] // heads
    shown = (iota((tokens, tokens), 0) <= iota((tokens, tokens), 1)) & (
        cols_ref[:, heads : heads + 1] == rows_ref[heads : heads + 1, :]
    )
    shown_ref[...] = jnp.where(shown, 0.0, -jnp.inf)
    total_ref[...] = jnp.zeros_like(total_ref)
    level = level_ref[0:1, :]
    for place in range(gq_ref.shape[1] // width):
        head = base + place
        at = slice(head * width, (head + 1) * width)
        to = slice(place * width, (place + 1) * width)
        q, k, v, o = q_ref[:, at], k_ref[:, at], v_ref[:, at], o_ref[:, at]
        gap = rows_ref[head : head + 1, :] - cols_ref[:, head : head + 1]
        within = jnp.exp(jnp.minimum(gap, shown_ref[...]))
        scores = dot(k, q, TURNED)
        shared = within * dot(v, o, TURNED)
        total_ref[...] += jnp.sum((shared * scores).reshape(tokens // 8, 8, tokens), axis=0)
        shared = shared * level
        gv_ref[:, to] = dot((within * level) * scores, o, ROWS)
        gk_ref[:, to] = dot(shared, q, ROWS)
        gq_ref[:, to] = dot(shared, k, COLS)
    own = jnp.sum(total_ref[...], axis=0, keepdims=True)
    terms = jnp.where(iota(terms_ref.shape, 0) == 0, own, 0.0)
    terms_ref[...] = terms if terms_in is None else terms + terms_in[...]


def factors_kernel(depth, device_ref, table_ref, factor_ref):
    stretches = table_ref.shape[0]
    device = device_ref[0]
    totals, lasts, firsts = table_ref[:, 0, :], table_ref[:, 1, :], table_ref[:, 2, :]
    stretch = iota((stretches, LANES), 0) ^ device

    def at(values, index):
        return jnp.sum(jnp.where(stretch == index, values, 0.0), axis=0, keepdims=True)

    def span(low, high):
        inside = (stretch > low) & (stretch <= high)
        return jnp.exp(jnp.sum(jnp.where(inside, totals, 0.0), axis=0, keepdims=True))

    def reach(low_end, target):
        return jnp.where(at(firsts, target) == at(lasts, low_end), span(low_end, target - 1), 0.0)

    factors = []
    for distance in range(depth):
        low_end = ((device >> (distance + 1)) << (distance + 1)) + (1 << distance) - 1
        upper = ((device >> distance) & 1) == 1
        factors.append(jnp.where(upper, reach(low_end, device), 0.0))
    for distance in range(depth):
        low_end = ((device >> (distance + 1)) << (distance + 1)) + (1 << distance) - 1
        high_end = low_end + (1 << distance)
        factors.append(
            jnp.where(at(lasts, low_end) == at(lasts, high_end), span(low_end, high_end), 0.0)
        )
    middle = stretches // 2 - 1
    second = device // (stretches // 4) == 1
    for hop in (stretches // 4, stretches // 2):
        target = jnp.minimum(device + hop, stretches - 1)
        factors.append(jnp.where(second, reach(middle, target), 0.0))
    factor_ref[...] = jnp.zeros_like(factor_ref)
    for index, factor in enumerate(factors):
        factor_ref[index : index + 1, :] = factor


def levels_kernel(heads, base, chosen, out_at, *refs):
    q_ref, uo_ref, spread_ref, factor_ref, gq_in, terms_in = refs[:6]
    blocks = refs[6 : 6 + len(chosen)]
    if out_at is None:
        gq_ref, terms_ref, *totals = refs[-(2 + len(chosen)) :]
    else:
        gq_hbm, terms_ref, *totals, gq_ref, sems = refs[-(4 + len(chosen)) :]
    copies = []
    width = spread_ref.shape[2]
    for place in range(gq_in.shape[1] // width):
        head = base + place
        at = slice(head * width, (head + 1) * width)
        to = slice(place * width, (place + 1) * width)
        states = [block[place] for block in blocks]
        states = [
            factor_ref[level - 1 : level, head : head + 1] * state
            for level, state in zip(chosen, states)
        ]
        q, uo = q_ref[:, at], uo_ref[:, at]
        reached = dot(q, jnp.concatenate(states, axis=1), ROWS)
        back = dot(uo, jnp.concatenate(states, axis=0), TURNED)
        gq = gq_in[:, to]
        for index, level in enumerate(chosen):
            here = slice(index * width, (index + 1) * width)
            gq = gq + spread_ref[level - 1] * back[:, here]
            term = reached[:, here] * uo
            totals[index][...] = term if place == 0 else totals[index][...] + term
        gq_ref[:, to] = gq
        if out_at is not None:
            copies.append(ship(gq_ref, gq_hbm, to, at, sems.at[place]))
    terms = terms_in[...]
    for total, level in zip(totals, chosen):
        row = jnp.sum(total[...].T, axis=0, keepdims=True)
        terms = terms + jnp.where(iota(terms.shape, 0) == level, row, 0.0)
    terms_ref[...] = terms
    for copy in copies:
        copy.wait()


def sources_kernel(heads, base, row, device_ref, wk_ref, wv_ref, factor_ref, kept_ref, came_ref, *refs):
    gk_in, gv_in = refs[:2]
    gk_hbm, gv_hbm, gk_ref, gv_ref, sems = refs[-5:]
    copies = []
    width = kept_ref.shape[2]
    upper = (device_ref[0] & 1).astype(jnp.float32)
    for place in range(gk_in.shape[1] // width):
        head = base + place
        at = slice(head * width, (head + 1) * width)
        to = slice(place * width, (place + 1) * width)
        own = upper + (1.0 - upper) * factor_ref[row : row + 1, head : head + 1]
        state = own * kept_ref[place] + came_ref[place]
        gk_ref[:, to] = gk_in[:, to] + dot(wv_ref[:, at], state, TURNED)
        copies.append(ship(gk_ref, gk_hbm, to, at, sems.at[0, place]))
        gv_ref[:, to] = gv_in[:, to] + dot(wk_ref[:, at], state, ROWS)
        copies.append(ship(gv_ref, gv_hbm, to, at, sems.at[1, place]))
    for copy in copies:
        copy.wait()


def blend_kernel(base, recipe, inputs, device_ref, factor_ref, *refs):
    arrays, out_ref = refs[:inputs], refs[-1]
    device = device_ref[0]
    factor = factor_ref[...]
    for place in range(out_ref.shape[0]):
        head = base + place
        column = factor[:, head : head + 1]
        total = None
        for array, coefficient in zip(arrays, recipe):
            weight = coefficient(device, lambda row: column[row : row + 1, :])
            term = array[place]
            term = term if weight is None else weight * term
            total = term if total is None else total + term
        out_ref[place] = total


def upper_flag(device, bit):
    return ((device >> bit) & 1).astype(jnp.float32)


def upper_or(bit, row):
    return lambda device, scalar: upper_flag(device, bit) * (1.0 - scalar(row)) + scalar(row)


def lower_or(bit, row):
    return lambda device, scalar: upper_flag(device, bit) * (scalar(row) - 1.0) + 1.0


def lower(bit):
    return lambda device, scalar: 1.0 - upper_flag(device, bit)


def quarter_flag(top, which, row=None):
    def weight(device, scalar):
        flag = (((device >> (top - 1)) & 3) == which).astype(jnp.float32)
        return flag if row is None else flag * scalar(row)

    return weight


def by(row):
    return lambda device, scalar: scalar(row)


def both(row, other):
    return lambda device, scalar: scalar(row) * scalar(other)


def plain(device, scalar):
    return None


def send(array, route):
    return lax.ppermute(array, "seq", route)


def on_device(queries, key_input, value_input, grad_output, log_decay, level_weight, segment):
    stretches = lax.axis_size("seq")
    depth = stretches.bit_length() - 1
    tokens, heads = log_decay.shape
    width = queries.shape[1] // heads
    levels = level_weight.shape[1]
    quarter = stretches // 4
    device = lax.axis_index("seq").astype(jnp.int32).reshape(1)
    part_heads = heads // PARTS
    parts = range(PARTS)
    part_width = part_heads * width
    factor_rows = -(-(2 * depth + 2) // 8) * 8
    side_rows = -(-(heads + 1) // 8) * 8
    turned_rows = -(-levels // 8) * 8
    token_bytes = tokens * width * 4
    work = 6 * tokens * width * width

    def shape(*dims):
        return jax.ShapeDtypeStruct(dims, jnp.float32)

    tall = shape(tokens, heads * width)
    state = shape(part_heads, width, width)
    decay_rows, level_rows = log_decay.T, level_weight.T
    swaps = [[(i, i ^ (1 << d)) for i in range(stretches)] for d in range(depth)]

    near_k, near_v, near_q, near_o, cols, rows, source, query, table = pl.pallas_call(
        functools.partial(first_kernel, heads),
        out_shape=[tall] * 4
        + [shape(tokens, LANES), shape(side_rows, tokens)]
        + [shape(heads, tokens)] * 2
        + [shape(1, 8, LANES)],
        in_specs=[SCALARS] + [FAR] * 6,
        out_specs=[WHOLE] * 9,
        scratch_shapes=[
            pltpu.VMEM((heads, tokens), jnp.float32),
            pltpu.VMEM((1, tokens), jnp.int32),
            pltpu.SemaphoreType.DMA((6,)),
        ],
        compiler_params=params(),
    )(
        device,
        *map(far, (decay_rows, segment.reshape(1, tokens))),
        *map(far, (key_input, value_input, queries, grad_output)),
    )

    weighted_o, spread, *grads = pl.pallas_call(
        functools.partial(second_kernel, heads, depth),
        out_shape=[tall, shape(depth, tokens, width)] + [state] * (PARTS * depth),
        in_specs=[WHOLE] * 4,
        out_specs=[WHOLE] * (2 + PARTS * depth),
        compiler_params=params(),
        cost_estimate=cost(heads * depth * work, heads * 2 * token_bytes),
    )(level_rows, *map(near, (query, near_q, near_o)))
    grads = [grads[p * depth : (p + 1) * depth] for p in parts]

    def join(table, d, after):
        return pl.pallas_call(
            join_kernel,
            out_shape=shape(2 << d, 8, LANES),
            in_specs=[WHOLE] * 2 + [ANYWHERE],
            out_specs=WHOLE,
            compiler_params=params(),
        )(near(table), near(send(table, swaps[d])), after)

    table = join(table, 0, weighted_o)

    weighted_k, weighted_v, *running = pl.pallas_call(
        functools.partial(states_kernel, heads),
        out_shape=[tall] * 2 + [state] * PARTS,
        in_specs=[WHOLE] * 3 + [ANYWHERE],
        out_specs=[WHOLE] * (2 + PARTS),
        compiler_params=params(),
        cost_estimate=cost(heads * work, 0),
    )(*map(near, (source, near_k, near_v)), table)


    gq, gk, gv = ([None] * PARTS for _ in range(3))
    terms = None
    for p in parts:
        before = [] if terms is None else [near(terms)]
        gq[p], gk[p], gv[p], terms = pl.pallas_call(
            functools.partial(local_kernel, heads, p * part_heads),
            out_shape=[shape(tokens, part_width)] * 3 + [shape(turned_rows, tokens)],
            in_specs=[WHOLE] * (7 + len(before)),
            out_specs=[WHOLE] * 4,
            scratch_shapes=[
                pltpu.VMEM((tokens, tokens), jnp.float32),
                pltpu.VMEM((8, tokens), jnp.float32),
            ],
            compiler_params=params(),
            cost_estimate=cost(part_heads * 30 * tokens * tokens * width, 0),
        )(*map(near, (near_q, near_k, near_v, near_o, cols, rows)), level_rows, *before)

    for d in range(1, depth):
        table = join(table, d, weighted_v if d == 1 else terms)
    factor = pl.pallas_call(
        functools.partial(factors_kernel, depth),
        out_shape=shape(factor_rows, LANES),
        in_specs=[SCALARS, WHOLE],
        out_specs=WHOLE,
        compiler_params=params(),
    )(device, near(table))

    def own_level(level):
        return level - 1

    def block_row(distance):
        return depth + distance

    third, fourth = 2 * depth, 2 * depth + 1
    second_third = [(quarter + i, 2 * quarter + i) for i in range(quarter)]
    third_fourth = [(2 * quarter + i, 3 * quarter + i) for i in range(quarter)]
    third_second = [(b, a) for a, b in second_third]
    shift_up = second_third + third_fourth
    shift_down = [(b, a) for a, b in shift_up]

    def add_levels(chosen, p, gq, terms, blocks, out=None, final=False):
        in_hbm = [] if out is None else [out]
        inputs = 6 + len(blocks)
        scratch = [pltpu.VMEM((tokens, width), jnp.float32)] * len(chosen)
        if final:
            scratch += [
                pltpu.VMEM((tokens, part_width), jnp.float32),
                pltpu.SemaphoreType.DMA((part_heads,)),
            ]
        return pl.pallas_call(
            functools.partial(
                levels_kernel,
                heads,
                p * part_heads,
                chosen,
                p if final else None,
            ),
            out_shape=[
                shape(tokens, heads * width if final else part_width),
                shape(turned_rows, tokens),
            ],
            in_specs=[WHOLE] * inputs + [FAR] * len(in_hbm),
            out_specs=[FAR if final else WHOLE, WHOLE],
            scratch_shapes=scratch,
            input_output_aliases={inputs: 0} if in_hbm else {},
            compiler_params=params(),
            cost_estimate=cost(part_heads * work * 2 * len(chosen), 0),
        )(*map(near, (near_q, weighted_o, spread, factor, gq, terms, *blocks)), *in_hbm)

    def blend(part, terms, after=()):
        arrays, recipe = zip(*terms)
        return pl.pallas_call(
            functools.partial(blend_kernel, part * part_heads, recipe, len(arrays)),
            out_shape=state,
            in_specs=[SCALARS, WHOLE] + [WHOLE] * len(arrays) + [ANYWHERE] * len(after),
            out_specs=WHOLE,
            compiler_params=params(),
            cost_estimate=cost(1, 1),
        )(device, *map(near, (factor, *arrays)), *after)

    top, next_bit = depth - 1, depth - 2
    shifted = [send(grads[p][top], shift_down) for p in parts]
    came = [[] for _ in parts]
    for d in range(depth - 2):
        for p in parts:
            arrived = send(running[p], swaps[d])
            came[p].append(arrived)
            running[p] = blend(
                p,
                [(running[p], upper_or(d, block_row(d))), (arrived, lower_or(d, block_row(d)))],
            )
    crossed, relayed, passed = [], [], []
    for p in parts:
        message = blend(
            p,
            [
                (running[p], lower(next_bit)),
                (grads[p][next_bit], by(own_level(depth - 1))),
                (shifted[p], both(block_row(next_bit), third)),
            ],
        )
        crossed.append(send(message, swaps[next_bit]))
        relayed.append(send(shifted[p], third_second))
        passed.append(send(running[p], second_third))
    if depth > 2:
        for p in parts:
            gq[p], terms = add_levels(list(range(1, depth - 1)), p, gq[p], terms, came[p])
    topmost, kept, sources = [], [], []
    for p in parts:
        upward = blend(
            p,
            [
                (running[p], quarter_flag(top, 1)),
                (crossed[p], quarter_flag(top, 1, block_row(next_bit))),
                (passed[p], quarter_flag(top, 2)),
            ],
            [terms],
        )
        topmost.append(send(upward, shift_up))
        pending = blend(
            p, [(crossed[p], lower(next_bit)), (shifted[p], by(third)), (relayed[p], by(fourth))]
        )
        for d in range(depth - 3, -1, -1):
            outgoing = blend(
                p, [(pending, lower_or(d, block_row(d))), (grads[p][d], by(own_level(d + 1)))]
            )
            arrived = send(outgoing, swaps[d])
            if d > 0:
                pending = blend(p, [(pending, upper_or(d, block_row(d))), (arrived, plain)])
        kept.append(pending)
        sources.append(arrived)
    for p in parts:
        gq[p], terms = add_levels([depth - 1], p, gq[p], terms, [crossed[p]])
    grad_query = None
    for p in parts:
        grad_query, terms = add_levels(
            [depth], p, gq[p], terms, [topmost[p]], grad_query, True
        )
    groups = lax.axis_size("head")
    others = [
        lax.ppermute(terms, "head", [(i, (i + k) % groups) for i in range(groups)])
        for k in range(1, groups)
    ]
    done = []
    for p in parts:
        done = pl.pallas_call(
            functools.partial(sources_kernel, heads, p * part_heads, block_row(0)),
            out_shape=[tall] * 2,
            in_specs=[SCALARS] + [WHOLE] * 7 + [FAR] * len(done),
            out_specs=[FAR] * 2,
            scratch_shapes=[pltpu.VMEM((tokens, part_width), jnp.float32)] * 2
            + [pltpu.SemaphoreType.DMA((2, part_heads))],
            input_output_aliases={8: 0, 9: 1} if done else {},
            compiler_params=params(),
            cost_estimate=cost(part_heads * work * 2, 0),
        )(
            device,
            *map(near, (weighted_k, weighted_v, factor, kept[p], sources[p], gk[p], gv[p])),
            *done,
        )
    grad_level = pl.pallas_call(
        total_kernel,
        out_shape=shape(levels, tokens),
        in_specs=[WHOLE] * groups,
        out_specs=WHOLE,
        compiler_params=params(),
    )(terms, *others)
    return grad_query, done[0], done[1], grad_level.T


def solution(mesh):
    in_specs = (
        P("seq", "head"),
        P("seq", "head"),
        P("seq", "head"),
        P("seq", "head"),
        P("seq", "head"),
        P("seq", None),
        P("seq"),
    )
    out_specs = (P("seq", "head"), P("seq", "head"), P("seq", "head"), P("seq", None))
    return jax.shard_map(
        on_device, mesh=mesh, in_specs=in_specs, out_specs=out_specs, check_vma=False
    )
```

```python
import functools

import jax
import jax.numpy as jnp
from jax import lax
from jax.experimental import pallas as pl
from jax.experimental.pallas import tpu as pltpu
from jax.sharding import PartitionSpec as P

HIGH = lax.Precision.HIGH
EXACT = lax.Precision.HIGHEST
LANES = 128
PARTS = 2
VMEM_LIMIT = 6 * 1024 * 1024
WHOLE = pl.BlockSpec(memory_space=pltpu.VMEM)
SCALARS = pl.BlockSpec(memory_space=pltpu.SMEM)
FAR = pl.BlockSpec(memory_space=pltpu.HBM)
ANYWHERE = pl.BlockSpec(memory_space=pl.ANY)
ROWS, COLS = ((1,), (0,)), ((0,), (0,))
TURNED = ((1,), (1,))


def dot(a, b, over, precision=HIGH):
    return lax.dot_general(
        a, b, (over, ((), ())), precision=precision, preferred_element_type=jnp.float32
    )


def params(steps=0):
    return pltpu.CompilerParams(
        dimension_semantics=("arbitrary",) * steps or None, vmem_limit_bytes=VMEM_LIMIT
    )


def cost(flops, moved):
    return pl.CostEstimate(flops=1, bytes_accessed=1, transcendentals=0)


def iota(shape, axis):
    return lax.broadcasted_iota(jnp.int32, shape, axis)


def near(array):
    return pltpu.with_memory_space_constraint(array, pltpu.VMEM)


def far(array):
    return pltpu.with_memory_space_constraint(array, pltpu.HBM)


def upright(row, width):
    return jnp.broadcast_to(row, (width, row.shape[1])).T


def ship(source, target, from_columns, to_columns, sem):
    copy = pltpu.make_async_copy(
        source.at[:, pl.ds(from_columns.start, from_columns.stop - from_columns.start)],
        target.at[:, pl.ds(to_columns.start, to_columns.stop - to_columns.start)],
        sem,
    )
    copy.start()
    return copy


def join_kernel(bit, device_ref, own_ref, came_ref, after_ref, out_ref):
    del after_ref
    half = own_ref.shape[0]
    upper = ((device_ref[0] >> bit) & 1) == 1
    out_ref[:half] = jnp.where(upper, came_ref[...], own_ref[...])
    out_ref[half:] = jnp.where(upper, own_ref[...], came_ref[...])


def rows_of(place, width):
    return slice(place * width, (place + 1) * width)


def total_kernel(*refs):
    total = refs[0][...]
    for ref in refs[1:-1]:
        total = total + ref[...]
    refs[-1][...] = total[: refs[-1].shape[0]]


def first_kernel(
    heads, device_ref, decay_hbm, segment_hbm, k_hbm, v_hbm, q_hbm, o_hbm, k_ref, v_ref, q_ref,
    o_ref, cols_ref, rows_ref, source_ref, query_ref, table_ref, decay_ref, segment_ref, sems,
):
    del device_ref
    tokens = segment_ref.shape[1]
    pairs = (
        (decay_hbm, decay_ref), (segment_hbm, segment_ref), (k_hbm, k_ref), (v_hbm, v_ref),
        (q_hbm, q_ref), (o_hbm, o_ref),
    )
    copies = [
        pltpu.make_async_copy(source, target, sems.at[index])
        for index, (source, target) in enumerate(pairs)
    ]
    for copy in copies:
        copy.start()
    copies[0].wait()
    copies[1].wait()
    sooner = iota((tokens, tokens), 0) <= iota((tokens, tokens), 1)
    running = dot(decay_ref[...], sooner.astype(jnp.float32), ROWS, EXACT)
    document = segment_ref[...].astype(jnp.float32)
    total, first, last = running[:, tokens - 1 :], document[:, :1], document[:, tokens - 1 :]
    source_ref[...] = jnp.exp(total - running) * (document == last).astype(jnp.float32)
    query_ref[...] = jnp.exp(running) * (document == first).astype(jnp.float32)
    spare = LANES - heads - 1
    rows = jnp.concatenate([running, document, jnp.zeros((spare, tokens), jnp.float32)], axis=0)
    rows_ref[...] = rows[: rows_ref.shape[0]]
    cols = rows.T
    cols_ref[...] = cols
    row = iota((8, LANES), 0)
    table_ref[...] = jnp.where(row == 0, cols[tokens - 1 :], jnp.where(row == 1, last, first))
    for copy in copies[2:]:
        copy.wait()


def states_kernel(heads, part_heads, source_ref, k_ref, v_ref, after_ref, wk_ref, wv_ref, *states):
    del after_ref
    width = k_ref.shape[1] // heads
    for head in range(heads):
        at = slice(head * width, (head + 1) * width)
        weight = upright(source_ref[head : head + 1, :], width)
        weighted = weight * k_ref[:, at]
        v = v_ref[:, at]
        wk_ref[:, at] = weighted
        wv_ref[:, at] = weight * v
        part, place = divmod(head, part_heads)
        states[part][rows_of(place, width), :] = dot(weighted, v, COLS)


def second_kernel(
    heads, depth, part_heads, level_ref, query_ref, q_ref, o_ref, table_ref, uo_ref, spread_ref, *outs
):
    width = q_ref.shape[1] // heads
    for d in range(depth):
        spread_ref[d] = upright(level_ref[d + 1 : d + 2, :], width)
    for head in range(heads):
        at = slice(head * width, (head + 1) * width)
        weight = upright(query_ref[head : head + 1, :], width)
        weighted = weight * o_ref[:, at]
        uo_ref[:, at] = weighted
        scaled = jnp.concatenate([spread_ref[d] * weighted for d in range(depth)], axis=1)
        grads = dot(q_ref[:, at], scaled, COLS)
        part, place = divmod(head, part_heads)
        for d in range(depth):
            outs[part * depth + d][rows_of(place, width), :] = grads[:, d * width : (d + 1) * width]
    for out in outs[depth - 1 :: depth]:
        out[part_heads * width :, :] = table_ref[...]


def local_kernel(
    heads, base, q_ref, k_ref, v_ref, o_ref, cols_ref, rows_ref, level_ref, *refs
):
    terms_in = refs[0] if base else None
    gq_ref, gk_ref, gv_ref, terms_ref, shown_ref, total_ref = refs[-6:]
    tokens = rows_ref.shape[1]
    width = k_ref.shape[1] // heads
    shown = (iota((tokens, tokens), 0) <= iota((tokens, tokens), 1)) & (
        cols_ref[:, heads : heads + 1] == rows_ref[heads : heads + 1, :]
    )
    shown_ref[...] = jnp.where(shown, 0.0, -jnp.inf)
    total_ref[...] = jnp.zeros_like(total_ref)
    level = level_ref[0:1, :]
    for place in range(gq_ref.shape[1] // width):
        head = base + place
        at = slice(head * width, (head + 1) * width)
        to = slice(place * width, (place + 1) * width)
        q, k, v, o = q_ref[:, at], k_ref[:, at], v_ref[:, at], o_ref[:, at]
        gap = rows_ref[head : head + 1, :] - cols_ref[:, head : head + 1]
        within = jnp.exp(jnp.minimum(gap, shown_ref[...]))
        scores = dot(k, q, TURNED)
        shared = within * dot(v, o, TURNED)
        total_ref[...] += jnp.sum((shared * scores).reshape(tokens // 8, 8, tokens), axis=0)
        shared = shared * level
        gv_ref[:, to] = dot((within * level) * scores, o, ROWS)
        gk_ref[:, to] = dot(shared, q, ROWS)
        gq_ref[:, to] = dot(shared, k, COLS)
    own = jnp.sum(total_ref[...], axis=0, keepdims=True)
    terms = jnp.where(iota(terms_ref.shape, 0) == 0, own, 0.0)
    terms_ref[...] = terms if terms_in is None else terms + terms_in[...]


def factors_kernel(depth, known, device_ref, *refs):
    own_ref, factor_ref, table_ref = refs[0], refs[-2], refs[-1]
    stretches = table_ref.shape[0]
    size = stretches // 4
    device = device_ref[0]
    quarter = device // size

    def put(where, values):
        @pl.when((where >= 0) & (where < 4))
        def _():
            table_ref[pl.ds(where * size, size)] = values.reshape(size, 8, LANES)

    table_ref[...] = jnp.zeros_like(table_ref)
    from_where = {
        "second": jnp.int32(1),
        "next": quarter + 1,
        "over": quarter + 2,
        "beside": quarter ^ 1,
    }
    for name, ref in zip(known, refs[1:-2]):
        put(from_where[name], ref[ref.shape[0] - 8 * size :, :])
    put(quarter, own_ref[...])
    totals, lasts, firsts = table_ref[:, 0, :], table_ref[:, 1, :], table_ref[:, 2, :]
    stretch = iota((stretches, LANES), 0)

    def at(values, index):
        return jnp.sum(jnp.where(stretch == index, values, 0.0), axis=0, keepdims=True)

    def span(low, high):
        inside = (stretch > low) & (stretch <= high)
        return jnp.exp(jnp.sum(jnp.where(inside, totals, 0.0), axis=0, keepdims=True))

    def reach(low_end, target):
        return jnp.where(at(firsts, target) == at(lasts, low_end), span(low_end, target - 1), 0.0)

    factors = []
    for distance in range(depth):
        low_end = ((device >> (distance + 1)) << (distance + 1)) + (1 << distance) - 1
        upper = ((device >> distance) & 1) == 1
        factors.append(jnp.where(upper, reach(low_end, device), 0.0))
    for distance in range(depth):
        low_end = ((device >> (distance + 1)) << (distance + 1)) + (1 << distance) - 1
        high_end = low_end + (1 << distance)
        factors.append(
            jnp.where(at(lasts, low_end) == at(lasts, high_end), span(low_end, high_end), 0.0)
        )
    middle = stretches // 2 - 1
    second = device // (stretches // 4) == 1
    for hop in (stretches // 4, stretches // 2):
        target = jnp.minimum(device + hop, stretches - 1)
        factors.append(jnp.where(second, reach(middle, target), 0.0))
    low_end = ((device >> (depth - 1)) << (depth - 1)) + size - 1
    upper = ((device >> (depth - 2)) & 1) == 1
    factors.append(jnp.where(upper, span(low_end, device - 1), 0.0))
    carried = jnp.where(
        at(firsts, device) == at(lasts, low_end + size), span(low_end, low_end + size), 0.0
    )
    factors.append(carried * factors[2 * depth])
    target = jnp.minimum(device + size, stretches - 1)
    linked = (at(firsts, target) == at(lasts, low_end)).astype(jnp.float32)
    factors.append(jnp.where(upper, 0.0, linked))
    factor_ref[...] = jnp.zeros_like(factor_ref)
    for index, factor in enumerate(factors):
        factor_ref[index : index + 1, :] = factor


def levels_kernel(heads, base, chosen, out_at, *refs):
    q_ref, uo_ref, spread_ref, factor_ref, gq_in, terms_in = refs[:6]
    blocks = refs[6 : 6 + len(chosen)]
    if out_at is None:
        gq_ref, terms_ref, *totals = refs[-(2 + len(chosen)) :]
    else:
        gq_hbm, terms_ref, *totals, gq_ref, sems = refs[-(4 + len(chosen)) :]
    copies = []
    width = spread_ref.shape[2]
    for place in range(gq_in.shape[1] // width):
        head = base + place
        at = slice(head * width, (head + 1) * width)
        to = slice(place * width, (place + 1) * width)
        states = [block[rows_of(place, width), :] for block in blocks]
        states = [
            factor_ref[level - 1 : level, head : head + 1] * state
            for level, state in zip(chosen, states)
        ]
        q, uo = q_ref[:, at], uo_ref[:, at]
        reached = dot(q, jnp.concatenate(states, axis=1), ROWS)
        back = dot(uo, jnp.concatenate(states, axis=0), TURNED)
        gq = gq_in[:, to]
        for index, level in enumerate(chosen):
            here = slice(index * width, (index + 1) * width)
            gq = gq + spread_ref[level - 1] * back[:, here]
            term = reached[:, here] * uo
            totals[index][...] = term if place == 0 else totals[index][...] + term
        gq_ref[:, to] = gq
        if out_at is not None:
            copies.append(ship(gq_ref, gq_hbm, to, at, sems.at[place]))
    terms = terms_in[...]
    for total, level in zip(totals, chosen):
        row = jnp.sum(total[...].T, axis=0, keepdims=True)
        terms = terms + jnp.where(iota(terms.shape, 0) == level, row, 0.0)
    terms_ref[...] = terms
    for copy in copies:
        copy.wait()


def sources_kernel(heads, base, row, device_ref, wk_ref, wv_ref, factor_ref, kept_ref, came_ref, *refs):
    gk_in, gv_in = refs[:2]
    gk_hbm, gv_hbm, gk_ref, gv_ref, sems = refs[-5:]
    copies = []
    width = kept_ref.shape[1]
    upper = (device_ref[0] & 1).astype(jnp.float32)
    for place in range(gk_in.shape[1] // width):
        head = base + place
        at = slice(head * width, (head + 1) * width)
        to = slice(place * width, (place + 1) * width)
        own = upper + (1.0 - upper) * factor_ref[row : row + 1, head : head + 1]
        state = own * kept_ref[rows_of(place, width), :] + came_ref[rows_of(place, width), :]
        gk_ref[:, to] = gk_in[:, to] + dot(wv_ref[:, at], state, TURNED)
        copies.append(ship(gk_ref, gk_hbm, to, at, sems.at[0, place]))
        gv_ref[:, to] = gv_in[:, to] + dot(wk_ref[:, at], state, ROWS)
        copies.append(ship(gv_ref, gv_hbm, to, at, sems.at[1, place]))
    for copy in copies:
        copy.wait()


def blend_kernel(base, recipe, inputs, relay, top, device_ref, factor_ref, table_ref, *refs):
    arrays, out_ref = refs[:inputs], refs[-1]
    device = device_ref[0]
    factor = factor_ref[...]
    width = out_ref.shape[1]
    states = out_ref.shape[0] - table_ref.shape[0]
    for place in range(states // width):
        column = factor[:, base + place : base + place + 1]
        total = None
        for array, coefficient in zip(arrays, recipe):
            weight = coefficient(device, lambda row: column[row : row + 1, :])
            term = array[rows_of(place, width), :]
            term = term if weight is None else weight * term
            total = term if total is None else total + term
        out_ref[rows_of(place, width), :] = total
    table = table_ref[...]
    if relay is not None:
        table = jnp.where(((device >> (top - 1)) & 3) == 2, arrays[relay][states:, :], table)
    out_ref[states:, :] = table


def upper_flag(device, bit):
    return ((device >> bit) & 1).astype(jnp.float32)


def upper_or(bit, row):
    return lambda device, scalar: upper_flag(device, bit) * (1.0 - scalar(row)) + scalar(row)


def lower_or(bit, row):
    return lambda device, scalar: upper_flag(device, bit) * (scalar(row) - 1.0) + 1.0


def lower(bit):
    return lambda device, scalar: 1.0 - upper_flag(device, bit)


def quarter_flag(top, which, row=None):
    def weight(device, scalar):
        flag = (((device >> (top - 1)) & 3) == which).astype(jnp.float32)
        return flag if row is None else flag * scalar(row)

    return weight


def by(row):
    return lambda device, scalar: scalar(row)


def both(row, other):
    return lambda device, scalar: scalar(row) * scalar(other)


def plain(device, scalar):
    return None


def send(array, route):
    return lax.ppermute(array, "seq", route)


def on_device(queries, key_input, value_input, grad_output, log_decay, level_weight, segment):
    stretches = lax.axis_size("seq")
    depth = stretches.bit_length() - 1
    tokens, heads = log_decay.shape
    width = queries.shape[1] // heads
    levels = level_weight.shape[1]
    quarter = stretches // 4
    device = lax.axis_index("seq").astype(jnp.int32).reshape(1)
    part_heads = heads // PARTS
    parts = range(PARTS)
    part_width = part_heads * width
    factor_rows = -(-(2 * depth + 5) // 8) * 8
    side_rows = -(-(heads + 1) // 8) * 8
    turned_rows = -(-levels // 8) * 8
    token_bytes = tokens * width * 4
    work = 6 * tokens * width * width

    def shape(*dims):
        return jax.ShapeDtypeStruct(dims, jnp.float32)

    tall = shape(tokens, heads * width)
    state = shape(part_heads * width + 8 * quarter, width)
    decay_rows, level_rows = log_decay.T, level_weight.T
    swaps = [[(i, i ^ (1 << d)) for i in range(stretches)] for d in range(depth)]

    near_k, near_v, near_q, near_o, cols, rows, source, query, table = pl.pallas_call(
        functools.partial(first_kernel, heads),
        out_shape=[tall] * 4
        + [shape(tokens, LANES), shape(side_rows, tokens)]
        + [shape(heads, tokens)] * 2
        + [shape(8, LANES)],
        in_specs=[SCALARS] + [FAR] * 6,
        out_specs=[WHOLE] * 9,
        scratch_shapes=[
            pltpu.VMEM((heads, tokens), jnp.float32),
            pltpu.VMEM((1, tokens), jnp.int32),
            pltpu.SemaphoreType.DMA((6,)),
        ],
        compiler_params=params(),
    )(
        device,
        *map(far, (decay_rows, segment.reshape(1, tokens))),
        *map(far, (key_input, value_input, queries, grad_output)),
    )

    gq, gk, gv = ([None] * PARTS for _ in range(3))
    terms = None
    for p in parts:
        before = [] if terms is None else [near(terms)]
        gq[p], gk[p], gv[p], terms = pl.pallas_call(
            functools.partial(local_kernel, heads, p * part_heads),
            out_shape=[shape(tokens, part_width)] * 3 + [shape(turned_rows, tokens)],
            in_specs=[WHOLE] * (7 + len(before)),
            out_specs=[WHOLE] * 4,
            scratch_shapes=[
                pltpu.VMEM((tokens, tokens), jnp.float32),
                pltpu.VMEM((8, tokens), jnp.float32),
            ],
            compiler_params=params(),
            cost_estimate=cost(part_heads * 30 * tokens * tokens * width, 0),
        )(*map(near, (near_q, near_k, near_v, near_o, cols, rows)), level_rows, *before)
        if p == 0:
            first_terms = terms

    for d in range(depth - 2):
        table = pl.pallas_call(
            functools.partial(join_kernel, d),
            out_shape=shape(16 << d, LANES),
            in_specs=[SCALARS] + [WHOLE] * 2 + [ANYWHERE],
            out_specs=WHOLE,
            compiler_params=params(),
        )(device, near(table), near(send(table, swaps[d])), first_terms)

    def factors(*known):
        names, arrays = [k[0] for k in known], [k[1] for k in known]
        return pl.pallas_call(
            functools.partial(factors_kernel, depth, names),
            out_shape=shape(factor_rows, LANES),
            in_specs=[SCALARS] + [WHOLE] * (1 + len(arrays)),
            out_specs=WHOLE,
            scratch_shapes=[pltpu.VMEM((stretches, 8, LANES), jnp.float32)],
            compiler_params=params(),
        )(device, *map(near, (table, *arrays)))

    weighted_k, weighted_v, *running = pl.pallas_call(
        functools.partial(states_kernel, heads, part_heads),
        out_shape=[tall] * 2 + [state] * PARTS,
        in_specs=[WHOLE] * 3 + [ANYWHERE],
        out_specs=[WHOLE] * (2 + PARTS),
        compiler_params=params(),
        cost_estimate=cost(heads * work, 0),
    )(*map(near, (source, near_k, near_v)), table)


    weighted_o, spread, *grads = pl.pallas_call(
        functools.partial(second_kernel, heads, depth, part_heads),
        out_shape=[tall, shape(depth, tokens, width)] + [state] * (PARTS * depth),
        in_specs=[WHOLE] * 5,
        out_specs=[WHOLE] * (2 + PARTS * depth),
        compiler_params=params(),
        cost_estimate=cost(heads * depth * work, heads * 2 * token_bytes),
    )(level_rows, *map(near, (query, near_q, near_o, table)))
    grads = [grads[p * depth : (p + 1) * depth] for p in parts]

    def own_level(level):
        return level - 1

    def block_row(distance):
        return depth + distance

    third, fourth, ahead, carried, linked = (2 * depth + i for i in range(5))
    second_third = [(quarter + i, 2 * quarter + i) for i in range(quarter)]
    third_fourth = [(2 * quarter + i, 3 * quarter + i) for i in range(quarter)]
    third_second = [(b, a) for a, b in second_third]
    shift_up = second_third + third_fourth
    shift_down = [(b, a) for a, b in shift_up]

    def add_levels(chosen, p, factor, gq, terms, blocks, out=None, final=False):
        in_hbm = [] if out is None else [out]
        inputs = 6 + len(blocks)
        scratch = [pltpu.VMEM((tokens, width), jnp.float32)] * len(chosen)
        if final:
            scratch += [
                pltpu.VMEM((tokens, part_width), jnp.float32),
                pltpu.SemaphoreType.DMA((part_heads,)),
            ]
        return pl.pallas_call(
            functools.partial(
                levels_kernel,
                heads,
                p * part_heads,
                chosen,
                p if final else None,
            ),
            out_shape=[
                shape(tokens, heads * width if final else part_width),
                shape(turned_rows, tokens),
            ],
            in_specs=[WHOLE] * inputs + [FAR] * len(in_hbm),
            out_specs=[FAR if final else WHOLE, WHOLE],
            scratch_shapes=scratch,
            input_output_aliases={inputs: 0} if in_hbm else {},
            compiler_params=params(),
            cost_estimate=cost(part_heads * work * 2 * len(chosen), 0),
        )(*map(near, (near_q, weighted_o, spread, factor, gq, terms, *blocks)), *in_hbm)

    top, next_bit = depth - 1, depth - 2

    def blend(part, factor, weighted, after=(), relay=None):
        arrays, recipe = zip(*weighted)
        return pl.pallas_call(
            functools.partial(
                blend_kernel, part * part_heads, recipe, len(arrays), relay, top
            ),
            out_shape=state,
            in_specs=[SCALARS] + [WHOLE] * (2 + len(arrays)) + [ANYWHERE] * len(after),
            out_specs=WHOLE,
            compiler_params=params(),
            cost_estimate=cost(1, 1),
        )(device, *map(near, (factor, table, *arrays)), *after)

    shifted = [send(grads[p][top], shift_down) for p in parts]
    came = [[] for _ in parts]
    inside = factors()
    for d in range(depth - 2):
        for p in parts:
            arrived = send(running[p], swaps[d])
            came[p].append(arrived)
            running[p] = blend(
                p,
                inside,
                [(running[p], upper_or(d, block_row(d))), (arrived, lower_or(d, block_row(d)))],
                [terms],
            )
    after_shift = factors(("next", shifted[0]))
    crossed, relayed, passed = [], [], []
    for p in parts:
        message = blend(
            p,
            after_shift,
            [
                (running[p], lower(next_bit)),
                (grads[p][next_bit], by(ahead)),
                (shifted[p], by(carried)),
            ],
        )
        crossed.append(send(message, swaps[next_bit]))
        relayed.append(send(shifted[p], third_second))
        passed.append(send(running[p], second_third))
    if depth > 2:
        for p in parts:
            gq[p], terms = add_levels(
                list(range(1, depth - 1)), p, inside, gq[p], terms, came[p]
            )
    after_cross = factors(("next", shifted[0]), ("beside", crossed[0]))
    after_relay = factors(("next", shifted[0]), ("over", relayed[0]), ("beside", crossed[0]))
    topmost, kept, sources = [], [], []
    for p in parts:
        upward = blend(
            p,
            after_cross,
            [
                (running[p], quarter_flag(top, 1)),
                (crossed[p], quarter_flag(top, 1, block_row(next_bit))),
                (passed[p], quarter_flag(top, 2)),
            ],
            [terms],
            2,
        )
        topmost.append(send(upward, shift_up))
        pending = blend(
            p,
            after_relay,
            [(crossed[p], by(linked)), (shifted[p], by(third)), (relayed[p], by(fourth))],
        )
        for d in range(depth - 3, -1, -1):
            outgoing = blend(
                p,
                inside,
                [(pending, lower_or(d, block_row(d))), (grads[p][d], by(own_level(d + 1)))],
            )
            arrived = send(outgoing, swaps[d])
            if d > 0:
                pending = blend(
                    p, inside, [(pending, upper_or(d, block_row(d))), (arrived, plain)]
                )
        kept.append(pending)
        sources.append(arrived)
    for p in parts:
        gq[p], terms = add_levels([depth - 1], p, after_cross, gq[p], terms, [crossed[p]])
    after_top = factors(("second", topmost[0]), ("beside", crossed[0]))
    grad_query = None
    for p in parts:
        grad_query, terms = add_levels(
            [depth], p, after_top, gq[p], terms, [topmost[p]], grad_query, True
        )
    groups = lax.axis_size("head")
    others = [
        lax.ppermute(terms, "head", [(i, (i + k) % groups) for i in range(groups)])
        for k in range(1, groups)
    ]
    done = []
    for p in parts:
        done = pl.pallas_call(
            functools.partial(sources_kernel, heads, p * part_heads, block_row(0)),
            out_shape=[tall] * 2,
            in_specs=[SCALARS] + [WHOLE] * 7 + [FAR] * len(done),
            out_specs=[FAR] * 2,
            scratch_shapes=[pltpu.VMEM((tokens, part_width), jnp.float32)] * 2
            + [pltpu.SemaphoreType.DMA((2, part_heads))],
            input_output_aliases={8: 0, 9: 1} if done else {},
            compiler_params=params(),
            cost_estimate=cost(part_heads * work * 2, 0),
        )(
            device,
            *map(near, (weighted_k, weighted_v, inside, kept[p], sources[p], gk[p], gv[p])),
            *done,
        )
    grad_level = pl.pallas_call(
        total_kernel,
        out_shape=shape(levels, tokens),
        in_specs=[WHOLE] * groups,
        out_specs=WHOLE,
        compiler_params=params(),
    )(terms, *others)
    return grad_query, done[0], done[1], grad_level.T


def solution(mesh):
    in_specs = (
        P("seq", "head"),
        P("seq", "head"),
        P("seq", "head"),
        P("seq", "head"),
        P("seq", "head"),
        P("seq", None),
        P("seq"),
    )
    out_specs = (P("seq", "head"), P("seq", "head"), P("seq", "head"), P("seq", None))
    return jax.shard_map(
        on_device, mesh=mesh, in_specs=in_specs, out_specs=out_specs, check_vma=False
    )
```

```python
import functools

import jax
import jax.numpy as jnp
from jax import lax
from jax.experimental import pallas as pl
from jax.experimental.pallas import tpu as pltpu
from jax.sharding import PartitionSpec as P

HIGH = lax.Precision.HIGH
EXACT = lax.Precision.HIGHEST
LANES = 128
PARTS = 2
VMEM_LIMIT = 6 * 1024 * 1024
WHOLE = pl.BlockSpec(memory_space=pltpu.VMEM)
SCALARS = pl.BlockSpec(memory_space=pltpu.SMEM)
FAR = pl.BlockSpec(memory_space=pltpu.HBM)
ANYWHERE = pl.BlockSpec(memory_space=pl.ANY)
ROWS, COLS = ((1,), (0,)), ((0,), (0,))
TURNED = ((1,), (1,))


def dot(a, b, over, precision=HIGH):
    return lax.dot_general(
        a, b, (over, ((), ())), precision=precision, preferred_element_type=jnp.float32
    )


def params(steps=0):
    return pltpu.CompilerParams(
        dimension_semantics=("arbitrary",) * steps or None, vmem_limit_bytes=VMEM_LIMIT
    )


def cost(flops, moved):
    return pl.CostEstimate(flops=1, bytes_accessed=1, transcendentals=0)


def iota(shape, axis):
    return lax.broadcasted_iota(jnp.int32, shape, axis)


def near(array):
    return pltpu.with_memory_space_constraint(array, pltpu.VMEM)


def far(array):
    return pltpu.with_memory_space_constraint(array, pltpu.HBM)


def upright(row, width):
    return jnp.broadcast_to(row, (width, row.shape[1])).T


def ship(source, target, from_columns, to_columns, sem):
    copy = pltpu.make_async_copy(
        source.at[:, pl.ds(from_columns.start, from_columns.stop - from_columns.start)],
        target.at[:, pl.ds(to_columns.start, to_columns.stop - to_columns.start)],
        sem,
    )
    copy.start()
    return copy


def join_kernel(bit, device_ref, own_ref, came_ref, after_ref, out_ref):
    del after_ref
    half = own_ref.shape[0]
    upper = ((device_ref[0] >> bit) & 1) == 1
    out_ref[:half] = jnp.where(upper, came_ref[...], own_ref[...])
    out_ref[half:] = jnp.where(upper, own_ref[...], came_ref[...])


def rows_of(place, width):
    return slice(place * width, (place + 1) * width)


def total_kernel(*refs):
    total = refs[0][...]
    for ref in refs[1:-1]:
        total = total + ref[...]
    refs[-1][...] = total[: refs[-1].shape[0]]


def first_kernel(
    heads, device_ref, decay_hbm, segment_hbm, k_hbm, v_hbm, q_hbm, o_hbm, k_ref, v_ref, q_ref,
    o_ref, cols_ref, rows_ref, source_ref, query_ref, table_ref, decay_ref, segment_ref, sems,
):
    del device_ref
    tokens = segment_ref.shape[1]
    pairs = (
        (decay_hbm, decay_ref), (segment_hbm, segment_ref), (k_hbm, k_ref), (v_hbm, v_ref),
        (q_hbm, q_ref), (o_hbm, o_ref),
    )
    copies = [
        pltpu.make_async_copy(source, target, sems.at[index])
        for index, (source, target) in enumerate(pairs)
    ]
    for copy in copies:
        copy.start()
    copies[0].wait()
    copies[1].wait()
    sooner = iota((tokens, tokens), 0) <= iota((tokens, tokens), 1)
    running = dot(decay_ref[...], sooner.astype(jnp.float32), ROWS, EXACT)
    document = segment_ref[...].astype(jnp.float32)
    total, first, last = running[:, tokens - 1 :], document[:, :1], document[:, tokens - 1 :]
    source_ref[...] = jnp.exp(total - running) * (document == last).astype(jnp.float32)
    query_ref[...] = jnp.exp(running) * (document == first).astype(jnp.float32)
    spare = LANES - heads - 1
    rows = jnp.concatenate([running, document, jnp.zeros((spare, tokens), jnp.float32)], axis=0)
    rows_ref[...] = rows[: rows_ref.shape[0]]
    cols = rows.T
    cols_ref[...] = cols
    row = iota((8, LANES), 0)
    table_ref[...] = jnp.where(row == 0, cols[tokens - 1 :], jnp.where(row == 1, last, first))
    for copy in copies[2:]:
        copy.wait()


def states_kernel(heads, part_heads, source_ref, k_ref, v_ref, after_ref, wk_ref, wv_ref, *states):
    del after_ref
    width = k_ref.shape[1] // heads
    for head in range(heads):
        at = slice(head * width, (head + 1) * width)
        weight = upright(source_ref[head : head + 1, :], width)
        weighted = weight * k_ref[:, at]
        v = v_ref[:, at]
        wk_ref[:, at] = weighted
        wv_ref[:, at] = weight * v
        part, place = divmod(head, part_heads)
        states[part][rows_of(place, width), :] = dot(weighted, v, COLS)


def second_kernel(
    heads, depth, part_heads, level_ref, query_ref, q_ref, o_ref, table_ref, uo_ref, spread_ref, *outs
):
    width = q_ref.shape[1] // heads
    for d in range(depth):
        spread_ref[d] = upright(level_ref[d + 1 : d + 2, :], width)
    for head in range(heads):
        at = slice(head * width, (head + 1) * width)
        weight = upright(query_ref[head : head + 1, :], width)
        weighted = weight * o_ref[:, at]
        uo_ref[:, at] = weighted
        scaled = jnp.concatenate([spread_ref[d] * weighted for d in range(depth)], axis=1)
        grads = dot(q_ref[:, at], scaled, COLS)
        part, place = divmod(head, part_heads)
        for d in range(depth):
            outs[part * depth + d][rows_of(place, width), :] = grads[:, d * width : (d + 1) * width]
    for out in outs[depth - 1 :: depth]:
        out[part_heads * width :, :] = table_ref[...]


def local_kernel(
    heads, base, q_ref, k_ref, v_ref, o_ref, cols_ref, rows_ref, level_ref, *refs
):
    terms_in = refs[0] if base else None
    gq_ref, gk_ref, gv_ref, terms_ref, shown_ref, total_ref = refs[-6:]
    tokens = rows_ref.shape[1]
    width = k_ref.shape[1] // heads
    shown = (iota((tokens, tokens), 0) <= iota((tokens, tokens), 1)) & (
        cols_ref[:, heads : heads + 1] == rows_ref[heads : heads + 1, :]
    )
    shown_ref[...] = jnp.where(shown, 0.0, -jnp.inf)
    total_ref[...] = jnp.zeros_like(total_ref)
    level = level_ref[0:1, :]
    for place in range(gq_ref.shape[1] // width):
        head = base + place
        at = slice(head * width, (head + 1) * width)
        to = slice(place * width, (place + 1) * width)
        q, k, v, o = q_ref[:, at], k_ref[:, at], v_ref[:, at], o_ref[:, at]
        gap = rows_ref[head : head + 1, :] - cols_ref[:, head : head + 1]
        within = jnp.exp(jnp.minimum(gap, shown_ref[...]))
        scores = dot(k, q, TURNED)
        shared = within * dot(v, o, TURNED)
        total_ref[...] += jnp.sum((shared * scores).reshape(tokens // 8, 8, tokens), axis=0)
        shared = shared * level
        gv_ref[:, to] = dot((within * level) * scores, o, ROWS)
        gk_ref[:, to] = dot(shared, q, ROWS)
        gq_ref[:, to] = dot(shared, k, COLS)
    own = jnp.sum(total_ref[...], axis=0, keepdims=True)
    terms = jnp.where(iota(terms_ref.shape, 0) == 0, own, 0.0)
    terms_ref[...] = terms if terms_in is None else terms + terms_in[...]


def factors_kernel(depth, known, device_ref, *refs):
    own_ref, factor_ref, table_ref = refs[0], refs[-2], refs[-1]
    stretches = table_ref.shape[0]
    size = stretches // 4
    device = device_ref[0]
    quarter = device // size

    def put(where, values):
        @pl.when((where >= 0) & (where < 4))
        def _():
            table_ref[pl.ds(where * size, size)] = values.reshape(size, 8, LANES)

    table_ref[...] = jnp.zeros_like(table_ref)
    from_where = {
        "second": jnp.int32(1),
        "next": quarter + 1,
        "over": quarter + 2,
        "beside": quarter ^ 1,
    }
    for name, ref in zip(known, refs[1:-2]):
        put(from_where[name], ref[ref.shape[0] - 8 * size :, :])
    put(quarter, own_ref[...])
    totals, lasts, firsts = table_ref[:, 0, :], table_ref[:, 1, :], table_ref[:, 2, :]
    stretch = iota((stretches, LANES), 0)

    def at(values, index):
        return jnp.sum(jnp.where(stretch == index, values, 0.0), axis=0, keepdims=True)

    def span(low, high):
        inside = (stretch > low) & (stretch <= high)
        return jnp.exp(jnp.sum(jnp.where(inside, totals, 0.0), axis=0, keepdims=True))

    def reach(low_end, target):
        return jnp.where(at(firsts, target) == at(lasts, low_end), span(low_end, target - 1), 0.0)

    factors = []
    for distance in range(depth):
        low_end = ((device >> (distance + 1)) << (distance + 1)) + (1 << distance) - 1
        upper = ((device >> distance) & 1) == 1
        factors.append(jnp.where(upper, reach(low_end, device), 0.0))
    for distance in range(depth):
        low_end = ((device >> (distance + 1)) << (distance + 1)) + (1 << distance) - 1
        high_end = low_end + (1 << distance)
        factors.append(
            jnp.where(at(lasts, low_end) == at(lasts, high_end), span(low_end, high_end), 0.0)
        )
    middle = stretches // 2 - 1
    second = device // (stretches // 4) == 1
    for hop in (stretches // 4, stretches // 2):
        target = jnp.minimum(device + hop, stretches - 1)
        factors.append(jnp.where(second, reach(middle, target), 0.0))
    low_end = ((device >> (depth - 1)) << (depth - 1)) + size - 1
    upper = ((device >> (depth - 2)) & 1) == 1
    factors.append(jnp.where(upper, span(low_end, device - 1), 0.0))
    carried = jnp.where(
        at(firsts, device) == at(lasts, low_end + size), span(low_end, low_end + size), 0.0
    )
    factors.append(carried * factors[2 * depth])
    target = jnp.minimum(device + size, stretches - 1)
    linked = (at(firsts, target) == at(lasts, low_end)).astype(jnp.float32)
    factors.append(jnp.where(upper, 0.0, linked))
    factor_ref[...] = jnp.zeros_like(factor_ref)
    for index, factor in enumerate(factors):
        factor_ref[index : index + 1, :] = factor


def levels_kernel(heads, base, chosen, out_at, *refs):
    q_ref, uo_ref, spread_ref, factor_ref, gq_in, terms_in = refs[:6]
    blocks = refs[6 : 6 + len(chosen)]
    if out_at is None:
        gq_ref, terms_ref, *totals = refs[-(2 + len(chosen)) :]
    else:
        gq_hbm, terms_ref, *totals, gq_ref, sems = refs[-(4 + len(chosen)) :]
    copies = []
    width = spread_ref.shape[2]
    for place in range(gq_in.shape[1] // width):
        head = base + place
        at = slice(head * width, (head + 1) * width)
        to = slice(place * width, (place + 1) * width)
        states = [block[rows_of(place, width), :] for block in blocks]
        states = [
            factor_ref[level - 1 : level, head : head + 1] * state
            for level, state in zip(chosen, states)
        ]
        q, uo = q_ref[:, at], uo_ref[:, at]
        reached = dot(q, jnp.concatenate(states, axis=1), ROWS)
        back = dot(uo, jnp.concatenate(states, axis=0), TURNED)
        gq = gq_in[:, to]
        for index, level in enumerate(chosen):
            here = slice(index * width, (index + 1) * width)
            gq = gq + spread_ref[level - 1] * back[:, here]
            term = reached[:, here] * uo
            totals[index][...] = term if place == 0 else totals[index][...] + term
        gq_ref[:, to] = gq
        if out_at is not None:
            copies.append(ship(gq_ref, gq_hbm, to, at, sems.at[place]))
    terms = terms_in[...]
    for total, level in zip(totals, chosen):
        row = jnp.sum(total[...].T, axis=0, keepdims=True)
        terms = terms + jnp.where(iota(terms.shape, 0) == level, row, 0.0)
    terms_ref[...] = terms
    for copy in copies:
        copy.wait()


def sources_kernel(heads, base, row, device_ref, wk_ref, wv_ref, factor_ref, kept_ref, came_ref, *refs):
    gk_in, gv_in = refs[:2]
    gk_hbm, gv_hbm, gk_ref, gv_ref, sems = refs[-5:]
    copies = []
    width = kept_ref.shape[1]
    upper = (device_ref[0] & 1).astype(jnp.float32)
    for place in range(gk_in.shape[1] // width):
        head = base + place
        at = slice(head * width, (head + 1) * width)
        to = slice(place * width, (place + 1) * width)
        own = upper + (1.0 - upper) * factor_ref[row : row + 1, head : head + 1]
        state = own * kept_ref[rows_of(place, width), :] + came_ref[rows_of(place, width), :]
        gk_ref[:, to] = gk_in[:, to] + dot(wv_ref[:, at], state, TURNED)
        copies.append(ship(gk_ref, gk_hbm, to, at, sems.at[0, place]))
        gv_ref[:, to] = gv_in[:, to] + dot(wk_ref[:, at], state, ROWS)
        copies.append(ship(gv_ref, gv_hbm, to, at, sems.at[1, place]))
    for copy in copies:
        copy.wait()


def blend_kernel(base, recipe, inputs, relay, top, device_ref, factor_ref, table_ref, *refs):
    arrays, out_ref = refs[:inputs], refs[-1]
    device = device_ref[0]
    factor = factor_ref[...]
    width = out_ref.shape[1]
    states = out_ref.shape[0] - table_ref.shape[0]
    for place in range(states // width):
        column = factor[:, base + place : base + place + 1]
        total = None
        for array, coefficient in zip(arrays, recipe):
            weight = coefficient(device, lambda row: column[row : row + 1, :])
            term = array[rows_of(place, width), :]
            term = term if weight is None else weight * term
            total = term if total is None else total + term
        out_ref[rows_of(place, width), :] = total
    table = table_ref[...]
    if relay is not None:
        table = jnp.where(((device >> (top - 1)) & 3) == 2, arrays[relay][states:, :], table)
    out_ref[states:, :] = table


def upper_flag(device, bit):
    return ((device >> bit) & 1).astype(jnp.float32)


def upper_or(bit, row):
    return lambda device, scalar: upper_flag(device, bit) * (1.0 - scalar(row)) + scalar(row)


def lower_or(bit, row):
    return lambda device, scalar: upper_flag(device, bit) * (scalar(row) - 1.0) + 1.0


def lower(bit):
    return lambda device, scalar: 1.0 - upper_flag(device, bit)


def quarter_flag(top, which, row=None):
    def weight(device, scalar):
        flag = (((device >> (top - 1)) & 3) == which).astype(jnp.float32)
        return flag if row is None else flag * scalar(row)

    return weight


def by(row):
    return lambda device, scalar: scalar(row)


def both(row, other):
    return lambda device, scalar: scalar(row) * scalar(other)


def plain(device, scalar):
    return None


def send(array, route):
    return lax.ppermute(array, "seq", route)


def on_device(queries, key_input, value_input, grad_output, log_decay, level_weight, segment):
    stretches = lax.axis_size("seq")
    depth = stretches.bit_length() - 1
    tokens, heads = log_decay.shape
    width = queries.shape[1] // heads
    levels = level_weight.shape[1]
    quarter = stretches // 4
    device = lax.axis_index("seq").astype(jnp.int32).reshape(1)
    part_heads = heads // PARTS
    parts = range(PARTS)
    part_width = part_heads * width
    factor_rows = -(-(2 * depth + 5) // 8) * 8
    side_rows = -(-(heads + 1) // 8) * 8
    turned_rows = -(-levels // 8) * 8
    token_bytes = tokens * width * 4
    work = 6 * tokens * width * width

    def shape(*dims):
        return jax.ShapeDtypeStruct(dims, jnp.float32)

    tall = shape(tokens, heads * width)
    state = shape(part_heads * width + 8 * quarter, width)
    decay_rows, level_rows = log_decay.T, level_weight.T
    swaps = [[(i, i ^ (1 << d)) for i in range(stretches)] for d in range(depth)]

    near_k, near_v, near_q, near_o, cols, rows, source, query, table = pl.pallas_call(
        functools.partial(first_kernel, heads),
        out_shape=[tall] * 4
        + [shape(tokens, LANES), shape(side_rows, tokens)]
        + [shape(heads, tokens)] * 2
        + [shape(8, LANES)],
        in_specs=[SCALARS] + [FAR] * 6,
        out_specs=[WHOLE] * 9,
        scratch_shapes=[
            pltpu.VMEM((heads, tokens), jnp.float32),
            pltpu.VMEM((1, tokens), jnp.int32),
            pltpu.SemaphoreType.DMA((6,)),
        ],
        compiler_params=params(),
    )(
        device,
        *map(far, (decay_rows, segment.reshape(1, tokens))),
        *map(far, (key_input, value_input, queries, grad_output)),
    )

    gq, gk, gv = ([None] * PARTS for _ in range(3))
    terms = None
    for p in parts:
        before = [] if terms is None else [near(terms)]
        gq[p], gk[p], gv[p], terms = pl.pallas_call(
            functools.partial(local_kernel, heads, p * part_heads),
            out_shape=[shape(tokens, part_width)] * 3 + [shape(turned_rows, tokens)],
            in_specs=[WHOLE] * (7 + len(before)),
            out_specs=[WHOLE] * 4,
            scratch_shapes=[
                pltpu.VMEM((tokens, tokens), jnp.float32),
                pltpu.VMEM((8, tokens), jnp.float32),
            ],
            compiler_params=params(),
            cost_estimate=cost(part_heads * 30 * tokens * tokens * width, 0),
        )(*map(near, (near_q, near_k, near_v, near_o, cols, rows)), level_rows, *before)
        if p == 0:
            first_terms = terms

    for d in range(depth - 2):
        table = pl.pallas_call(
            functools.partial(join_kernel, d),
            out_shape=shape(16 << d, LANES),
            in_specs=[SCALARS] + [WHOLE] * 2 + [ANYWHERE],
            out_specs=WHOLE,
            compiler_params=params(),
        )(device, near(table), near(send(table, swaps[d])), first_terms)

    def factors(*known):
        names, arrays = [k[0] for k in known], [k[1] for k in known]
        return pl.pallas_call(
            functools.partial(factors_kernel, depth, names),
            out_shape=shape(factor_rows, LANES),
            in_specs=[SCALARS] + [WHOLE] * (1 + len(arrays)),
            out_specs=WHOLE,
            scratch_shapes=[pltpu.VMEM((stretches, 8, LANES), jnp.float32)],
            compiler_params=params(),
        )(device, *map(near, (table, *arrays)))

    weighted_k, weighted_v, *running = pl.pallas_call(
        functools.partial(states_kernel, heads, part_heads),
        out_shape=[tall] * 2 + [state] * PARTS,
        in_specs=[WHOLE] * 3 + [ANYWHERE],
        out_specs=[WHOLE] * (2 + PARTS),
        compiler_params=params(),
        cost_estimate=cost(heads * work, 0),
    )(*map(near, (source, near_k, near_v)), table)


    weighted_o, spread, *grads = pl.pallas_call(
        functools.partial(second_kernel, heads, depth, part_heads),
        out_shape=[tall, shape(depth, tokens, width)] + [state] * (PARTS * depth),
        in_specs=[WHOLE] * 5,
        out_specs=[WHOLE] * (2 + PARTS * depth),
        compiler_params=params(),
        cost_estimate=cost(heads * depth * work, heads * 2 * token_bytes),
    )(level_rows, *map(near, (query, near_q, near_o, table)))
    grads = [grads[p * depth : (p + 1) * depth] for p in parts]

    def own_level(level):
        return level - 1

    def block_row(distance):
        return depth + distance

    third, fourth, ahead, carried, linked = (2 * depth + i for i in range(5))
    second_third = [(quarter + i, 2 * quarter + i) for i in range(quarter)]
    third_fourth = [(2 * quarter + i, 3 * quarter + i) for i in range(quarter)]
    third_second = [(b, a) for a, b in second_third]
    shift_up = second_third + third_fourth
    shift_down = [(b, a) for a, b in shift_up]

    def add_levels(chosen, p, factor, gq, terms, blocks, out=None, final=False):
        in_hbm = [] if out is None else [out]
        inputs = 6 + len(blocks)
        scratch = [pltpu.VMEM((tokens, width), jnp.float32)] * len(chosen)
        if final:
            scratch += [
                pltpu.VMEM((tokens, part_width), jnp.float32),
                pltpu.SemaphoreType.DMA((part_heads,)),
            ]
        return pl.pallas_call(
            functools.partial(
                levels_kernel,
                heads,
                p * part_heads,
                chosen,
                p if final else None,
            ),
            out_shape=[
                shape(tokens, heads * width if final else part_width),
                shape(turned_rows, tokens),
            ],
            in_specs=[WHOLE] * inputs + [FAR] * len(in_hbm),
            out_specs=[FAR if final else WHOLE, WHOLE],
            scratch_shapes=scratch,
            input_output_aliases={inputs: 0} if in_hbm else {},
            compiler_params=params(),
            cost_estimate=cost(part_heads * work * 2 * len(chosen), 0),
        )(*map(near, (near_q, weighted_o, spread, factor, gq, terms, *blocks)), *in_hbm)

    top, next_bit = depth - 1, depth - 2

    def blend(part, factor, weighted, after=(), relay=None):
        arrays, recipe = zip(*weighted)
        return pl.pallas_call(
            functools.partial(
                blend_kernel, part * part_heads, recipe, len(arrays), relay, top
            ),
            out_shape=state,
            in_specs=[SCALARS] + [WHOLE] * (2 + len(arrays)) + [ANYWHERE] * len(after),
            out_specs=WHOLE,
            compiler_params=params(),
            cost_estimate=cost(1, 1),
        )(device, *map(near, (factor, table, *arrays)), *after)

    shifted = [send(grads[p][top], shift_down) for p in parts]
    came = [[] for _ in parts]
    inside = factors()
    for d in range(depth - 2):
        for p in parts:
            arrived = send(running[p], swaps[d])
            came[p].append(arrived)
            running[p] = blend(
                p,
                inside,
                [(running[p], upper_or(d, block_row(d))), (arrived, lower_or(d, block_row(d)))],
                [terms],
            )
    after_shift = factors(("next", shifted[0]))
    crossed, middle = [], []
    for p in parts:
        message = blend(
            p,
            after_shift,
            [
                (running[p], lower(next_bit)),
                (grads[p][next_bit], by(ahead)),
                (shifted[p], by(carried)),
            ],
        )
        crossed.append(send(message, swaps[next_bit]))
        payload = blend(
            p,
            after_shift,
            [(running[p], quarter_flag(top, 1)), (shifted[p], quarter_flag(top, 2))],
            relay=1,
        )
        middle.append(send(payload, second_third + third_second))
    if depth > 2:
        for p in parts:
            gq[p], terms = add_levels(
                list(range(1, depth - 1)), p, inside, gq[p], terms, came[p]
            )
    after_cross = factors(("next", shifted[0]), ("beside", crossed[0]))
    after_relay = factors(("next", shifted[0]), ("over", middle[0]), ("beside", crossed[0]))
    topmost, kept, sources = [], [], []
    for p in parts:
        upward = blend(
            p,
            after_cross,
            [
                (running[p], quarter_flag(top, 1)),
                (crossed[p], quarter_flag(top, 1, block_row(next_bit))),
                (middle[p], quarter_flag(top, 2)),
            ],
            [terms],
            2,
        )
        topmost.append(send(upward, shift_up))
        pending = blend(
            p,
            after_relay,
            [(crossed[p], by(linked)), (shifted[p], by(third)), (middle[p], by(fourth))],
        )
        for d in range(depth - 3, -1, -1):
            outgoing = blend(
                p,
                inside,
                [(pending, lower_or(d, block_row(d))), (grads[p][d], by(own_level(d + 1)))],
            )
            arrived = send(outgoing, swaps[d])
            if d > 0:
                pending = blend(
                    p, inside, [(pending, upper_or(d, block_row(d))), (arrived, plain)]
                )
        kept.append(pending)
        sources.append(arrived)
    for p in parts:
        gq[p], terms = add_levels([depth - 1], p, after_cross, gq[p], terms, [crossed[p]])
    after_top = factors(("second", topmost[0]), ("beside", crossed[0]))
    grad_query = None
    for p in parts:
        grad_query, terms = add_levels(
            [depth], p, after_top, gq[p], terms, [topmost[p]], grad_query, True
        )
    groups = lax.axis_size("head")
    others = [
        lax.ppermute(terms, "head", [(i, (i + k) % groups) for i in range(groups)])
        for k in range(1, groups)
    ]
    done = []
    for p in parts:
        done = pl.pallas_call(
            functools.partial(sources_kernel, heads, p * part_heads, block_row(0)),
            out_shape=[tall] * 2,
            in_specs=[SCALARS] + [WHOLE] * 7 + [FAR] * len(done),
            out_specs=[FAR] * 2,
            scratch_shapes=[pltpu.VMEM((tokens, part_width), jnp.float32)] * 2
            + [pltpu.SemaphoreType.DMA((2, part_heads))],
            input_output_aliases={8: 0, 9: 1} if done else {},
            compiler_params=params(),
            cost_estimate=cost(part_heads * work * 2, 0),
        )(
            device,
            *map(near, (weighted_k, weighted_v, inside, kept[p], sources[p], gk[p], gv[p])),
            *done,
        )
    grad_level = pl.pallas_call(
        total_kernel,
        out_shape=shape(levels, tokens),
        in_specs=[WHOLE] * groups,
        out_specs=WHOLE,
        compiler_params=params(),
    )(terms, *others)
    return grad_query, done[0], done[1], grad_level.T


def solution(mesh):
    in_specs = (
        P("seq", "head"),
        P("seq", "head"),
        P("seq", "head"),
        P("seq", "head"),
        P("seq", "head"),
        P("seq", None),
        P("seq"),
    )
    out_specs = (P("seq", "head"), P("seq", "head"), P("seq", "head"), P("seq", None))
    return jax.shard_map(
        on_device, mesh=mesh, in_specs=in_specs, out_specs=out_specs, check_vma=False
    )
```

```python
import functools

import jax
import jax.numpy as jnp
from jax import lax
from jax.experimental import pallas as pl
from jax.experimental.pallas import tpu as pltpu
from jax.sharding import PartitionSpec as P

HIGH = lax.Precision.HIGH
EXACT = lax.Precision.HIGHEST
LANES = 128
PARTS = 2
VMEM_LIMIT = 6 * 1024 * 1024
WHOLE = pl.BlockSpec(memory_space=pltpu.VMEM)
SCALARS = pl.BlockSpec(memory_space=pltpu.SMEM)
FAR = pl.BlockSpec(memory_space=pltpu.HBM)
ANYWHERE = pl.BlockSpec(memory_space=pl.ANY)
ROWS, COLS = ((1,), (0,)), ((0,), (0,))
TURNED = ((1,), (1,))


def dot(a, b, over, precision=HIGH):
    return lax.dot_general(
        a, b, (over, ((), ())), precision=precision, preferred_element_type=jnp.float32
    )


def params(steps=0):
    return pltpu.CompilerParams(
        dimension_semantics=("arbitrary",) * steps or None, vmem_limit_bytes=VMEM_LIMIT
    )


def cost(flops, moved):
    return pl.CostEstimate(flops=1, bytes_accessed=1, transcendentals=0)


def iota(shape, axis):
    return lax.broadcasted_iota(jnp.int32, shape, axis)


def near(array):
    return pltpu.with_memory_space_constraint(array, pltpu.VMEM)


def far(array):
    return pltpu.with_memory_space_constraint(array, pltpu.HBM)


def upright(row, width):
    return jnp.broadcast_to(row, (width, row.shape[1])).T


def ship(source, target, from_columns, to_columns, sem):
    copy = pltpu.make_async_copy(
        source.at[:, pl.ds(from_columns.start, from_columns.stop - from_columns.start)],
        target.at[:, pl.ds(to_columns.start, to_columns.stop - to_columns.start)],
        sem,
    )
    copy.start()
    return copy


def join_kernel(bit, device_ref, own_ref, came_ref, after_ref, out_ref):
    del after_ref
    half = own_ref.shape[0]
    upper = ((device_ref[0] >> bit) & 1) == 1
    out_ref[:half] = jnp.where(upper, came_ref[...], own_ref[...])
    out_ref[half:] = jnp.where(upper, own_ref[...], came_ref[...])


def rows_of(place, width):
    return slice(place * width, (place + 1) * width)


def total_kernel(*refs):
    total = refs[0][...]
    for ref in refs[1:-1]:
        total = total + ref[...]
    refs[-1][...] = total[: refs[-1].shape[0]]


def first_kernel(
    heads, device_ref, decay_hbm, segment_hbm, k_hbm, v_hbm, q_hbm, o_hbm, k_ref, v_ref, q_ref,
    o_ref, cols_ref, rows_ref, source_ref, query_ref, table_ref, decay_ref, segment_ref, sems,
):
    del device_ref
    tokens = segment_ref.shape[1]
    pairs = (
        (decay_hbm, decay_ref), (segment_hbm, segment_ref), (k_hbm, k_ref), (v_hbm, v_ref),
        (q_hbm, q_ref), (o_hbm, o_ref),
    )
    copies = [
        pltpu.make_async_copy(source, target, sems.at[index])
        for index, (source, target) in enumerate(pairs)
    ]
    for copy in copies:
        copy.start()
    copies[0].wait()
    copies[1].wait()
    sooner = iota((tokens, tokens), 0) <= iota((tokens, tokens), 1)
    running = dot(decay_ref[...], sooner.astype(jnp.float32), ROWS, EXACT)
    document = segment_ref[...].astype(jnp.float32)
    total, first, last = running[:, tokens - 1 :], document[:, :1], document[:, tokens - 1 :]
    source_ref[...] = jnp.exp(total - running) * (document == last).astype(jnp.float32)
    query_ref[...] = jnp.exp(running) * (document == first).astype(jnp.float32)
    spare = LANES - heads - 1
    rows = jnp.concatenate([running, document, jnp.zeros((spare, tokens), jnp.float32)], axis=0)
    rows_ref[...] = rows[: rows_ref.shape[0]]
    cols = rows.T
    cols_ref[...] = cols
    row = iota((8, LANES), 0)
    table_ref[...] = jnp.where(row == 0, cols[tokens - 1 :], jnp.where(row == 1, last, first))
    for copy in copies[2:]:
        copy.wait()


def states_kernel(heads, part_heads, source_ref, k_ref, v_ref, after_ref, wk_ref, wv_ref, *states):
    del after_ref
    width = k_ref.shape[1] // heads
    for head in range(heads):
        at = slice(head * width, (head + 1) * width)
        weight = upright(source_ref[head : head + 1, :], width)
        weighted = weight * k_ref[:, at]
        v = v_ref[:, at]
        wk_ref[:, at] = weighted
        wv_ref[:, at] = weight * v
        part, place = divmod(head, part_heads)
        states[part][rows_of(place, width), :] = dot(weighted, v, COLS)


def second_kernel(
    heads, depth, part_heads, level_ref, query_ref, q_ref, o_ref, table_ref, uo_ref, spread_ref, *outs
):
    width = q_ref.shape[1] // heads
    for d in range(depth):
        spread_ref[d] = upright(level_ref[d + 1 : d + 2, :], width)
    for head in range(heads):
        at = slice(head * width, (head + 1) * width)
        weight = upright(query_ref[head : head + 1, :], width)
        weighted = weight * o_ref[:, at]
        uo_ref[:, at] = weighted
        scaled = jnp.concatenate([spread_ref[d] * weighted for d in range(depth)], axis=1)
        grads = dot(q_ref[:, at], scaled, COLS)
        part, place = divmod(head, part_heads)
        for d in range(depth):
            outs[part * depth + d][rows_of(place, width), :] = grads[:, d * width : (d + 1) * width]
    for out in outs[depth - 1 :: depth]:
        out[part_heads * width :, :] = table_ref[...]


def local_kernel(
    heads, base, q_ref, k_ref, v_ref, o_ref, cols_ref, rows_ref, level_ref, *refs
):
    terms_in = refs[0] if base else None
    gq_ref, gk_ref, gv_ref, terms_ref, shown_ref, total_ref = refs[-6:]
    tokens = rows_ref.shape[1]
    width = k_ref.shape[1] // heads
    shown = (iota((tokens, tokens), 0) <= iota((tokens, tokens), 1)) & (
        cols_ref[:, heads : heads + 1] == rows_ref[heads : heads + 1, :]
    )
    shown_ref[...] = jnp.where(shown, 0.0, -jnp.inf)
    total_ref[...] = jnp.zeros_like(total_ref)
    level = level_ref[0:1, :]
    for place in range(gq_ref.shape[1] // width):
        head = base + place
        at = slice(head * width, (head + 1) * width)
        to = slice(place * width, (place + 1) * width)
        q, k, v, o = q_ref[:, at], k_ref[:, at], v_ref[:, at], o_ref[:, at]
        gap = rows_ref[head : head + 1, :] - cols_ref[:, head : head + 1]
        within = jnp.exp(jnp.minimum(gap, shown_ref[...]))
        scores = dot(k, q, TURNED)
        shared = within * dot(v, o, TURNED)
        total_ref[...] += jnp.sum((shared * scores).reshape(tokens // 8, 8, tokens), axis=0)
        shared = shared * level
        gv_ref[:, to] = dot((within * level) * scores, o, ROWS)
        gk_ref[:, to] = dot(shared, q, ROWS)
        gq_ref[:, to] = dot(shared, k, COLS)
    own = jnp.sum(total_ref[...], axis=0, keepdims=True)
    terms = jnp.where(iota(terms_ref.shape, 0) == 0, own, 0.0)
    terms_ref[...] = terms if terms_in is None else terms + terms_in[...]


def factors_kernel(depth, known, device_ref, *refs):
    own_ref, factor_ref, table_ref = refs[0], refs[-2], refs[-1]
    stretches = table_ref.shape[0]
    size = stretches // 4
    device = device_ref[0]
    quarter = device // size

    def put(where, values):
        @pl.when((where >= 0) & (where < 4))
        def _():
            table_ref[pl.ds(where * size, size)] = values.reshape(size, 8, LANES)

    table_ref[...] = jnp.zeros_like(table_ref)
    from_where = {
        "second": jnp.int32(1),
        "next": quarter + 1,
        "over": quarter + 2,
        "beside": quarter ^ 1,
    }
    for name, ref in zip(known, refs[1:-2]):
        put(from_where[name], ref[ref.shape[0] - 8 * size :, :])
    put(quarter, own_ref[...])
    totals, lasts, firsts = table_ref[:, 0, :], table_ref[:, 1, :], table_ref[:, 2, :]
    stretch = iota((stretches, LANES), 0)

    def at(values, index):
        return jnp.sum(jnp.where(stretch == index, values, 0.0), axis=0, keepdims=True)

    def span(low, high):
        inside = (stretch > low) & (stretch <= high)
        return jnp.exp(jnp.sum(jnp.where(inside, totals, 0.0), axis=0, keepdims=True))

    def reach(low_end, target):
        return jnp.where(at(firsts, target) == at(lasts, low_end), span(low_end, target - 1), 0.0)

    factors = []
    for distance in range(depth):
        low_end = ((device >> (distance + 1)) << (distance + 1)) + (1 << distance) - 1
        upper = ((device >> distance) & 1) == 1
        factors.append(jnp.where(upper, reach(low_end, device), 0.0))
    for distance in range(depth):
        low_end = ((device >> (distance + 1)) << (distance + 1)) + (1 << distance) - 1
        high_end = low_end + (1 << distance)
        factors.append(
            jnp.where(at(lasts, low_end) == at(lasts, high_end), span(low_end, high_end), 0.0)
        )
    middle = stretches // 2 - 1
    second = device // (stretches // 4) == 1
    for hop in (stretches // 4, stretches // 2):
        target = jnp.minimum(device + hop, stretches - 1)
        factors.append(jnp.where(second, reach(middle, target), 0.0))
    low_end = ((device >> (depth - 1)) << (depth - 1)) + size - 1
    upper = ((device >> (depth - 2)) & 1) == 1
    factors.append(jnp.where(upper, span(low_end, device - 1), 0.0))
    carried = jnp.where(
        at(firsts, device) == at(lasts, low_end + size), span(low_end, low_end + size), 0.0
    )
    factors.append(carried * factors[2 * depth])
    target = jnp.minimum(device + size, stretches - 1)
    linked = (at(firsts, target) == at(lasts, low_end)).astype(jnp.float32)
    factors.append(jnp.where(upper, 0.0, linked))
    factor_ref[...] = jnp.zeros_like(factor_ref)
    for index, factor in enumerate(factors):
        factor_ref[index : index + 1, :] = factor


def levels_kernel(heads, base, chosen, out_at, *refs):
    q_ref, uo_ref, spread_ref, factor_ref, gq_in, terms_in = refs[:6]
    blocks = refs[6 : 6 + len(chosen)]
    if out_at is None:
        gq_ref, terms_ref, *totals = refs[-(2 + len(chosen)) :]
    else:
        gq_hbm, terms_ref, *totals, gq_ref, sems = refs[-(4 + len(chosen)) :]
    copies = []
    width = spread_ref.shape[2]
    for place in range(gq_in.shape[1] // width):
        head = base + place
        at = slice(head * width, (head + 1) * width)
        to = slice(place * width, (place + 1) * width)
        states = [block[rows_of(place, width), :] for block in blocks]
        states = [
            factor_ref[level - 1 : level, head : head + 1] * state
            for level, state in zip(chosen, states)
        ]
        q, uo = q_ref[:, at], uo_ref[:, at]
        reached = dot(q, jnp.concatenate(states, axis=1), ROWS)
        back = dot(uo, jnp.concatenate(states, axis=0), TURNED)
        gq = gq_in[:, to]
        for index, level in enumerate(chosen):
            here = slice(index * width, (index + 1) * width)
            gq = gq + spread_ref[level - 1] * back[:, here]
            term = reached[:, here] * uo
            totals[index][...] = term if place == 0 else totals[index][...] + term
        gq_ref[:, to] = gq
        if out_at is not None:
            copies.append(ship(gq_ref, gq_hbm, to, at, sems.at[place]))
    terms = terms_in[...]
    for total, level in zip(totals, chosen):
        row = jnp.sum(total[...].T, axis=0, keepdims=True)
        terms = terms + jnp.where(iota(terms.shape, 0) == level, row, 0.0)
    terms_ref[...] = terms
    for copy in copies:
        copy.wait()


def sources_kernel(heads, base, row, device_ref, wk_ref, wv_ref, factor_ref, kept_ref, came_ref, *refs):
    gk_in, gv_in = refs[:2]
    gk_hbm, gv_hbm, gk_ref, gv_ref, sems = refs[-5:]
    copies = []
    width = kept_ref.shape[1]
    upper = (device_ref[0] & 1).astype(jnp.float32)
    for place in range(gk_in.shape[1] // width):
        head = base + place
        at = slice(head * width, (head + 1) * width)
        to = slice(place * width, (place + 1) * width)
        own = upper + (1.0 - upper) * factor_ref[row : row + 1, head : head + 1]
        state = own * kept_ref[rows_of(place, width), :] + came_ref[rows_of(place, width), :]
        gk_ref[:, to] = gk_in[:, to] + dot(wv_ref[:, at], state, TURNED)
        copies.append(ship(gk_ref, gk_hbm, to, at, sems.at[0, place]))
        gv_ref[:, to] = gv_in[:, to] + dot(wk_ref[:, at], state, ROWS)
        copies.append(ship(gv_ref, gv_hbm, to, at, sems.at[1, place]))
    for copy in copies:
        copy.wait()


def blend_kernel(base, recipe, inputs, relay, top, device_ref, factor_ref, table_ref, *refs):
    arrays, out_ref = refs[:inputs], refs[-1]
    device = device_ref[0]
    factor = factor_ref[...]
    width = out_ref.shape[1]
    states = out_ref.shape[0] - table_ref.shape[0]
    for place in range(states // width):
        column = factor[:, base + place : base + place + 1]
        total = None
        for array, coefficient in zip(arrays, recipe):
            weight = coefficient(device, lambda row: column[row : row + 1, :])
            term = array[rows_of(place, width), :]
            term = term if weight is None else weight * term
            total = term if total is None else total + term
        out_ref[rows_of(place, width), :] = total
    table = table_ref[...]
    if relay is not None:
        table = jnp.where(((device >> (top - 1)) & 3) == 2, arrays[relay][states:, :], table)
    out_ref[states:, :] = table


def upper_flag(device, bit):
    return ((device >> bit) & 1).astype(jnp.float32)


def upper_or(bit, row):
    return lambda device, scalar: upper_flag(device, bit) * (1.0 - scalar(row)) + scalar(row)


def lower_or(bit, row):
    return lambda device, scalar: upper_flag(device, bit) * (scalar(row) - 1.0) + 1.0


def lower(bit):
    return lambda device, scalar: 1.0 - upper_flag(device, bit)


def quarter_flag(top, which, row=None):
    def weight(device, scalar):
        flag = (((device >> (top - 1)) & 3) == which).astype(jnp.float32)
        return flag if row is None else flag * scalar(row)

    return weight


def by(row):
    return lambda device, scalar: scalar(row)


def both(row, other):
    return lambda device, scalar: scalar(row) * scalar(other)


def plain(device, scalar):
    return None


def send(array, route):
    return lax.ppermute(array, "seq", route)


def on_device(queries, key_input, value_input, grad_output, log_decay, level_weight, segment):
    stretches = lax.axis_size("seq")
    depth = stretches.bit_length() - 1
    tokens, heads = log_decay.shape
    width = queries.shape[1] // heads
    levels = level_weight.shape[1]
    quarter = stretches // 4
    device = lax.axis_index("seq").astype(jnp.int32).reshape(1)
    part_heads = heads // PARTS
    parts = range(PARTS)
    part_width = part_heads * width
    factor_rows = -(-(2 * depth + 5) // 8) * 8
    side_rows = -(-(heads + 1) // 8) * 8
    turned_rows = -(-levels // 8) * 8
    token_bytes = tokens * width * 4
    work = 6 * tokens * width * width

    def shape(*dims):
        return jax.ShapeDtypeStruct(dims, jnp.float32)

    tall = shape(tokens, heads * width)
    state = shape(part_heads * width + 8 * quarter, width)
    decay_rows, level_rows = log_decay.T, level_weight.T
    swaps = [[(i, i ^ (1 << d)) for i in range(stretches)] for d in range(depth)]

    near_k, near_v, near_q, near_o, cols, rows, source, query, table = pl.pallas_call(
        functools.partial(first_kernel, heads),
        out_shape=[tall] * 4
        + [shape(tokens, LANES), shape(side_rows, tokens)]
        + [shape(heads, tokens)] * 2
        + [shape(8, LANES)],
        in_specs=[SCALARS] + [FAR] * 6,
        out_specs=[WHOLE] * 9,
        scratch_shapes=[
            pltpu.VMEM((heads, tokens), jnp.float32),
            pltpu.VMEM((1, tokens), jnp.int32),
            pltpu.SemaphoreType.DMA((6,)),
        ],
        compiler_params=params(),
    )(
        device,
        *map(far, (decay_rows, segment.reshape(1, tokens))),
        *map(far, (key_input, value_input, queries, grad_output)),
    )

    gq, gk, gv = ([None] * PARTS for _ in range(3))
    terms = None
    for p in parts:
        before = [] if terms is None else [near(terms)]
        gq[p], gk[p], gv[p], terms = pl.pallas_call(
            functools.partial(local_kernel, heads, p * part_heads),
            out_shape=[shape(tokens, part_width)] * 3 + [shape(turned_rows, tokens)],
            in_specs=[WHOLE] * (7 + len(before)),
            out_specs=[WHOLE] * 4,
            scratch_shapes=[
                pltpu.VMEM((tokens, tokens), jnp.float32),
                pltpu.VMEM((8, tokens), jnp.float32),
            ],
            compiler_params=params(),
            cost_estimate=cost(part_heads * 30 * tokens * tokens * width, 0),
        )(*map(near, (near_q, near_k, near_v, near_o, cols, rows)), level_rows, *before)
        if p == 0:
            first_terms = terms

    for d in range(depth - 2):
        table = pl.pallas_call(
            functools.partial(join_kernel, d),
            out_shape=shape(16 << d, LANES),
            in_specs=[SCALARS] + [WHOLE] * 2 + [ANYWHERE],
            out_specs=WHOLE,
            compiler_params=params(),
        )(device, near(table), near(send(table, swaps[d])), first_terms)

    def factors(*known):
        names, arrays = [k[0] for k in known], [k[1] for k in known]
        return pl.pallas_call(
            functools.partial(factors_kernel, depth, names),
            out_shape=shape(factor_rows, LANES),
            in_specs=[SCALARS] + [WHOLE] * (1 + len(arrays)),
            out_specs=WHOLE,
            scratch_shapes=[pltpu.VMEM((stretches, 8, LANES), jnp.float32)],
            compiler_params=params(),
        )(device, *map(near, (table, *arrays)))

    weighted_k, weighted_v, *running = pl.pallas_call(
        functools.partial(states_kernel, heads, part_heads),
        out_shape=[tall] * 2 + [state] * PARTS,
        in_specs=[WHOLE] * 3 + [ANYWHERE],
        out_specs=[WHOLE] * (2 + PARTS),
        compiler_params=params(),
        cost_estimate=cost(heads * work, 0),
    )(*map(near, (source, near_k, near_v)), table)


    weighted_o, spread, *grads = pl.pallas_call(
        functools.partial(second_kernel, heads, depth, part_heads),
        out_shape=[tall, shape(depth, tokens, width)] + [state] * (PARTS * depth),
        in_specs=[WHOLE] * 5,
        out_specs=[WHOLE] * (2 + PARTS * depth),
        compiler_params=params(),
        cost_estimate=cost(heads * depth * work, heads * 2 * token_bytes),
    )(level_rows, *map(near, (query, near_q, near_o, table)))
    grads = [grads[p * depth : (p + 1) * depth] for p in parts]

    def own_level(level):
        return level - 1

    def block_row(distance):
        return depth + distance

    third, fourth, ahead, carried, linked = (2 * depth + i for i in range(5))
    second_third = [(quarter + i, 2 * quarter + i) for i in range(quarter)]
    third_fourth = [(2 * quarter + i, 3 * quarter + i) for i in range(quarter)]
    third_second = [(b, a) for a, b in second_third]
    shift_up = second_third + third_fourth
    shift_down = [(b, a) for a, b in shift_up]

    def add_levels(chosen, p, factor, gq, terms, blocks, out=None, final=False):
        in_hbm = [] if out is None else [out]
        inputs = 6 + len(blocks)
        scratch = [pltpu.VMEM((tokens, width), jnp.float32)] * len(chosen)
        if final:
            scratch += [
                pltpu.VMEM((tokens, part_width), jnp.float32),
                pltpu.SemaphoreType.DMA((part_heads,)),
            ]
        return pl.pallas_call(
            functools.partial(
                levels_kernel,
                heads,
                p * part_heads,
                chosen,
                p if final else None,
            ),
            out_shape=[
                shape(tokens, heads * width if final else part_width),
                shape(turned_rows, tokens),
            ],
            in_specs=[WHOLE] * inputs + [FAR] * len(in_hbm),
            out_specs=[FAR if final else WHOLE, WHOLE],
            scratch_shapes=scratch,
            input_output_aliases={inputs: 0} if in_hbm else {},
            compiler_params=params(),
            cost_estimate=cost(part_heads * work * 2 * len(chosen), 0),
        )(*map(near, (near_q, weighted_o, spread, factor, gq, terms, *blocks)), *in_hbm)

    top, next_bit = depth - 1, depth - 2

    def blend(part, factor, weighted, after=(), relay=None):
        arrays, recipe = zip(*weighted)
        return pl.pallas_call(
            functools.partial(
                blend_kernel, part * part_heads, recipe, len(arrays), relay, top
            ),
            out_shape=state,
            in_specs=[SCALARS] + [WHOLE] * (2 + len(arrays)) + [ANYWHERE] * len(after),
            out_specs=WHOLE,
            compiler_params=params(),
            cost_estimate=cost(1, 1),
        )(device, *map(near, (factor, table, *arrays)), *after)

    shifted = [send(grads[p][top], shift_down) for p in parts]
    came = [[] for _ in parts]
    inside = factors()
    for d in range(depth - 2):
        for p in parts:
            arrived = send(running[p], swaps[d])
            came[p].append(arrived)
            running[p] = blend(
                p,
                inside,
                [(running[p], upper_or(d, block_row(d))), (arrived, lower_or(d, block_row(d)))],
                [terms],
            )
    after_shift = factors(("next", shifted[0]))
    crossed, middle = [], []
    for p in parts:
        message = blend(
            p,
            after_shift,
            [
                (running[p], lower(next_bit)),
                (grads[p][next_bit], by(ahead)),
                (shifted[p], by(carried)),
            ],
        )
        crossed.append(send(message, swaps[next_bit]))
        payload = blend(
            p,
            after_shift,
            [(running[p], quarter_flag(top, 1)), (shifted[p], quarter_flag(top, 2))],
            relay=1,
        )
        middle.append(send(payload, second_third + third_second))
    if depth > 2:
        for p in parts:
            gq[p], terms = add_levels(
                list(range(1, depth - 1)), p, inside, gq[p], terms, came[p]
            )
    after_cross = factors(("next", shifted[0]), ("beside", crossed[0]))
    after_relay = factors(("next", shifted[0]), ("over", middle[0]), ("beside", crossed[0]))
    topmost, kept, sources = [], [], []
    for p in parts:
        upward = blend(
            p,
            after_cross,
            [
                (running[p], quarter_flag(top, 1)),
                (crossed[p], quarter_flag(top, 1, block_row(next_bit))),
                (middle[p], quarter_flag(top, 2)),
            ],
            [terms],
            2,
        )
        topmost.append(send(upward, shift_up))
        pending = blend(
            p,
            after_relay,
            [(crossed[p], by(linked)), (shifted[p], by(third)), (middle[p], by(fourth))],
        )
        for d in range(depth - 3, -1, -1):
            outgoing = blend(
                p,
                inside,
                [(pending, lower_or(d, block_row(d))), (grads[p][d], by(own_level(d + 1)))],
            )
            arrived = send(outgoing, swaps[d])
            if d > 0:
                pending = blend(
                    p, inside, [(pending, upper_or(d, block_row(d))), (arrived, plain)]
                )
        kept.append(pending)
        sources.append(arrived)
    for p in parts:
        gq[p], terms = add_levels([depth - 1], p, after_cross, gq[p], terms, [crossed[p]])
    after_top = factors(("second", topmost[0]), ("beside", crossed[0]))
    grad_query = None
    for p in parts:
        grad_query, terms = add_levels(
            [depth], p, after_top, gq[p], terms, [topmost[p]], grad_query, True
        )
    done = []
    for p in parts:
        done = pl.pallas_call(
            functools.partial(sources_kernel, heads, p * part_heads, block_row(0)),
            out_shape=[tall] * 2,
            in_specs=[SCALARS] + [WHOLE] * 7 + [FAR] * len(done),
            out_specs=[FAR] * 2,
            scratch_shapes=[pltpu.VMEM((tokens, part_width), jnp.float32)] * 2
            + [pltpu.SemaphoreType.DMA((2, part_heads))],
            input_output_aliases={8: 0, 9: 1} if done else {},
            compiler_params=params(),
            cost_estimate=cost(part_heads * work * 2, 0),
        )(
            device,
            *map(near, (weighted_k, weighted_v, inside, kept[p], sources[p], gk[p], gv[p])),
            *done,
        )
    groups = lax.axis_size("head")
    bits = groups.bit_length() - 1
    grad_level = terms
    for bit in range(bits):
        other = lax.ppermute(grad_level, "head", [(i, i ^ (1 << bit)) for i in range(groups)])
        grad_level = pl.pallas_call(
            total_kernel,
            out_shape=shape(levels if bit == bits - 1 else turned_rows, tokens),
            in_specs=[WHOLE] * 2,
            out_specs=WHOLE,
            compiler_params=params(),
        )(grad_level, other)
    return grad_query, done[0], done[1], grad_level.T


def solution(mesh):
    in_specs = (
        P("seq", "head"),
        P("seq", "head"),
        P("seq", "head"),
        P("seq", "head"),
        P("seq", "head"),
        P("seq", None),
        P("seq"),
    )
    out_specs = (P("seq", "head"), P("seq", "head"), P("seq", "head"), P("seq", None))
    return jax.shard_map(
        on_device, mesh=mesh, in_specs=in_specs, out_specs=out_specs, check_vma=False
    )
```
